256 devices in a mesh: slab: 8 (over y, core), angle: 32 (over z, x).
Axes of the slice: x: 4, y: 4, z: 8, core: 2. Of those that a mesh axis runs over, the one named last changes fastest.
Arguments:
- volume: float32 [8192, 128], P(('slab', 'angle')), may hold values from -6 to 6
- measured: float32 [2048, 128], P('angle'), may hold values from 30 to 1000
- footprint: bfloat16 [49152, 128, 128], P(('slab', 'angle')), may hold values from 0.0099487305 to 1
- block_voxel: int32 [49152], P(('slab', 'angle')), may hold values from 0 to 1023, as said below
- block_tile: int32 [49152], P(('slab', 'angle')), may hold values from 0 to 63
- block_rows: int32 [49152], P(('slab', 'angle')), may hold values from 0 to 128, as said below
Outputs:
- new_volume: float32 [8192, 128], P(('slab', 'angle'))
- weighted_residual: float32 [2048, 128], P('angle')
The draws below stay inside these ranges and needn't reach their ends.
Inputs may be any that keep to these rules, and one draw needn't show every extreme that they name: `block_rows`: 0 marks an empty slot; the live slots of each device come first, each device has at least 48 live slots, some device has all 192 live, and every device has a live slot covering all 128 rows. On each device the slots form aligned groups of 12 in a row whose voxel blocks all lie in one share block_voxel // 32, different groups of a device in different shares; so at most 12 slots of a device name one share, and in each slab one share is named by 12 slots of every device.
All inputs are finite; a program needn't handle non-finite values.
Results may differ from the reference program's by a relative error of at most 0.00042.
Values may be sent and summed in bfloat16 or wider, within the bound.
No kernel may reach another device: no remote copies, remote signals or barrier semaphores. Data moves between devices by JAX's collectives and lax.ppermute only.
A program may use at most 64 MiB of HBM per device.

```python
import math
import jax
import jax.numpy as jnp
from jax import lax

BLK = 128
VBD = 32
PTD = 64
NB = 192
CAP = 12
VB_SLAB = 1024
VBLOCKS = 8192
TILES = 2048
SLOTS = 49152
N_SLAB = 8
N_ANGLE = 32


def draw_block_rows(key, part):
    key = jax.random.fold_in(key, 7)
    key_rows, key_full, key_live, key_busy = jax.random.split(key, 4)
    device_count = SLOTS // NB
    slot_ids = jnp.arange(NB, dtype=jnp.int32)
    counts = jax.random.randint(key_rows, (device_count, NB), 1, BLK + 1)
    full_slot = jax.random.randint(key_full, (device_count,), 0, NB // 4)
    counts = jnp.where(slot_ids[None, :] == full_slot[:, None], BLK, counts)
    live_slots = jax.random.randint(key_live, (device_count,), NB // 4, NB + 1)
    busiest = jax.random.randint(key_busy, (), 0, device_count)
    live_slots = jnp.where(jnp.arange(device_count, dtype=jnp.int32) == busiest, NB, live_slots)
    counts = jnp.where(slot_ids[None, :] < live_slots[:, None], counts, 0)
    return counts.reshape(SLOTS).astype(jnp.int32)


def draw_block_voxel(key, part):
    key = jax.random.fold_in(key, 11)
    key_common, key_order, key_within = jax.random.split(key, 3)
    device_count = SLOTS // NB
    group_count = NB // CAP
    common = jax.random.randint(key_common, (), 0, N_ANGLE)
    order_keys = jax.random.split(key_order, device_count)
    shuffled = jax.vmap(lambda k: jax.random.permutation(k, N_ANGLE - 1))(order_keys).astype(jnp.int32) + 1
    offsets = jnp.concatenate([jnp.zeros((device_count, 1), jnp.int32), shuffled], 1)[:, :group_count]
    owners = (common + offsets) % N_ANGLE
    owner_slot = jnp.repeat(owners, CAP, axis=1)
    within = jax.random.randint(key_within, (device_count, NB), 0, VBD)
    return (owner_slot * VBD + within).reshape(SLOTS).astype(jnp.int32)


def with_ends(entries, stream_key, smallest, high):
    longest = entries.shape.index(max(entries.shape))
    spots = []
    for shift in (0, 1):
        where = [jax.random.randint(jax.random.fold_in(stream_key, axis), (), 0, length) for axis, length in enumerate(entries.shape)]
        where[longest] = (where[longest] + shift) % entries.shape[longest]
        spots.append(tuple(where))
    return entries.at[spots[0]].set(smallest).at[spots[1]].set(high)


def block_levels(rng, dims, cuts, smallest, largest):
    loudness, own = 1.0, jax.random.fold_in(rng, 6)
    for dim, blocks in cuts:
        steps = jnp.exp(jax.random.uniform(jax.random.fold_in(own, dim), (blocks,), jnp.float32, smallest / len(cuts), largest / len(cuts)))
        loudness = loudness * jnp.repeat(steps, dims[dim] // blocks).reshape([-1 if axis == dim else 1 for axis in range(len(dims))])
    return loudness


def bell_draw(own_key, dims, spread, limit, pieces=(), kind=jnp.bfloat16):
    entries = spread * jax.random.normal(own_key, dims, jnp.float32)
    if pieces:
        entries = entries * block_levels(own_key, dims, pieces, -0.22, 0.18)
    return jnp.clip(entries, -limit, limit).astype(kind)


def setup_inputs(seed: int = 0) -> dict:
    arg_keys = jax.random.split(jax.random.key(seed), 7)
    volume = bell_draw(arg_keys[0], (VBLOCKS, BLK), 1.0, 6.0, ((0, 256),), jnp.float32)
    measured = jnp.clip(jnp.exp(math.log(1000.0) - 3.506558 * jax.random.uniform(arg_keys[1], (TILES, BLK), jnp.float32) ** block_levels(arg_keys[1], (TILES, BLK), ((0, 32),), -0.2, 0.2)), 30.0, 1000.0)
    footprint = jnp.clip(jnp.exp(math.log(1.0) - 4.61031033 * jax.random.uniform(arg_keys[2], (SLOTS, BLK, BLK), jnp.float32) ** block_levels(arg_keys[2], (SLOTS, BLK, BLK), ((0, 256),), -0.2, 0.2)), 0.0099487305, 1.0).astype(jnp.bfloat16)
    block_voxel = draw_block_voxel(jax.random.fold_in(arg_keys[6], 71), 0)
    block_tile = with_ends(jax.random.randint(arg_keys[4], (SLOTS,), 0, PTD), jax.random.fold_in(arg_keys[4], 1), 0, PTD - 1).astype(jnp.int32)
    block_rows = draw_block_rows(jax.random.fold_in(arg_keys[6], 71), 0)
    return {"volume": volume, "measured": measured, "footprint": footprint, "block_voxel": block_voxel, "block_tile": block_tile, "block_rows": block_rows}


def reference(volume, measured, footprint, block_voxel, block_tile, block_rows):
    device_count = N_SLAB * N_ANGLE
    owner = jnp.arange(SLOTS, dtype=jnp.int32) // NB
    glob_voxel = ((owner // N_ANGLE) * VB_SLAB + block_voxel).astype(jnp.int32)
    glob_tile = ((owner % N_ANGLE) * PTD + block_tile).astype(jnp.int32)
    row_live = (jnp.arange(BLK, dtype=jnp.int32)[None, :] < block_rows[:, None]).astype(jnp.float32)
    coarse = lax.optimization_barrier(volume.astype(jnp.bfloat16)).astype(jnp.float32)
    mats_all = footprint.reshape(device_count, NB, BLK, BLK)
    voxels_all = glob_voxel.reshape(device_count, NB)
    tiles_all = glob_tile.reshape(device_count, NB)
    live_all = row_live.reshape(device_count, NB, BLK)

    def forward_step(total, items):
        mats, voxels, tiles, live_rows = items
        picked = coarse[voxels]
        stacked = jnp.stack([picked, jnp.ones_like(picked)], 1)
        contrib = jnp.einsum('bpv,bkv->bkp', mats.astype(jnp.float32), stacked, precision=lax.Precision.HIGHEST)
        contrib = contrib * live_rows[:, None, :]
        return total.at[tiles].add(contrib), None

    totals, _ = lax.scan(forward_step, jnp.zeros((TILES, 2, BLK), jnp.float32), (mats_all, voxels_all, tiles_all, live_all))
    weighted = (measured - totals[:, 0]) / jnp.maximum(totals[:, 1], 1.0)
    coarse_res = lax.optimization_barrier(weighted.astype(jnp.bfloat16)).astype(jnp.float32)

    def backward_step(total, items):
        mats, voxels, tiles, live_rows = items
        picked = coarse_res[tiles] * live_rows
        stacked = jnp.stack([picked, live_rows], 1)
        contrib = jnp.einsum('bpv,bkp->bkv', mats.astype(jnp.float32), stacked, precision=lax.Precision.HIGHEST)
        return total.at[voxels].add(contrib), None

    backs, _ = lax.scan(backward_step, jnp.zeros((VBLOCKS, 2, BLK), jnp.float32), (mats_all, voxels_all, tiles_all, live_all))
    correction = backs[:, 0] / jnp.maximum(backs[:, 1], 1.0)
    return volume + correction, weighted
```

```python
import jax
import jax.numpy as jnp
from jax import lax
from jax.experimental import pallas as pl
from jax.experimental.pallas import tpu as pltpu
from jax.sharding import PartitionSpec as P

BLK = 128
NB = 192
CAP = 12
GROUP = 16
F32 = jnp.float32
BF16 = jnp.bfloat16
VMEM = pl.BlockSpec(memory_space=pltpu.VMEM)
SMEM = pl.BlockSpec(memory_space=pltpu.SMEM)
PARAMS = pltpu.CompilerParams(vmem_limit_bytes=40 * 1024 * 1024)


def dot(a, b, contract=((1,), (0,))):
    return lax.dot_general(a, b, (contract, ((), ())), preferred_element_type=F32)


def split3(x):
    hi = x.astype(BF16)
    rest = x - hi.astype(F32)
    mid = rest.astype(BF16)
    lo = (rest - mid.astype(F32)).astype(BF16)
    return jnp.concatenate([hi, mid, lo], axis=1)


def exact_dot(onehot, x):
    n = x.shape[1]
    y = dot(onehot, split3(x))
    return y[:, :n] + (y[:, n : 2 * n] + y[:, 2 * n :])


def forward_kernel(slab_ref, voxel_hot_ref, tile_hot_t_ref, live_ref, foot_ref, part_ref, slots):
    values = slab_ref[:, 0:32, :].reshape(1024, BLK)
    picked = dot(voxel_hot_ref[...], values).astype(BF16)
    slots[:, 0:BLK] = picked.astype(F32)
    row = lax.broadcasted_iota(jnp.int32, (GROUP, BLK), 0)
    ones = jnp.ones((GROUP, BLK), BF16)

    @pl.loop(0, NB // GROUP)
    def _(g):
        at = pl.ds(pl.multiple_of(g * GROUP, GROUP), GROUP)
        lhs = jnp.concatenate([slots[at, 0:BLK].astype(BF16), ones], axis=0)
        proj = jnp.zeros((GROUP, BLK), F32)
        rsum = jnp.zeros((GROUP, BLK), F32)
        for i in range(GROUP):
            out = dot(lhs, foot_ref[g * GROUP + i], ((1,), (1,)))
            proj = jnp.where(row == i, out[:GROUP], proj)
            rsum = jnp.where(row == i, out[GROUP:], rsum)
        live = live_ref[at, :].astype(F32)
        slots[at, 0:BLK] = proj * live
        slots[at, BLK:] = rsum * live

    part_ref[...] = exact_dot(tile_hot_t_ref[...], slots[...])


def backward_kernel(share_ref, parts_ref, measured_ref, tile_hot_ref, live_ref, foot_ref, weighted_ref, send_ref, rows, backs):
    total = jnp.sum(parts_ref[...], axis=0)
    weighted = (measured_ref[...] - total[:, :BLK]) / jnp.maximum(total[:, BLK:], 1.0)
    weighted_ref[...] = weighted
    rows[...] = dot(tile_hot_ref[...], weighted.astype(BF16))
    row = lax.broadcasted_iota(jnp.int32, (GROUP, BLK), 0)

    @pl.loop(0, NB // GROUP)
    def _(g):
        at = pl.ds(pl.multiple_of(g * GROUP, GROUP), GROUP)
        live = live_ref[at, :].astype(F32)
        res = rows[at, :] * live
        diag = jnp.concatenate(
            [
                jnp.concatenate([jnp.where(row == i, res, 0.0), jnp.where(row == i, live, 0.0)], axis=0)
                for i in range(GROUP)
            ],
            axis=1,
        ).astype(BF16)
        foot = foot_ref[pl.ds(g * GROUP, GROUP)].reshape(GROUP * BLK, BLK)
        out = dot(diag, foot)
        backs[0, at, :] = out[:GROUP]
        backs[1, at, :] = out[GROUP:]

    send_ref[...] = jnp.zeros_like(send_ref)
    for j in range(NB // CAP):
        share = share_ref[j]
        send_ref[share, 0:CAP, :] = backs[0, CAP * j : CAP * (j + 1), :]
        send_ref[share, CAP : 2 * CAP, :] = backs[1, CAP * j : CAP * (j + 1), :]


def update_kernel(recv_ref, hot_ref, volume_ref, out_ref):
    received = recv_ref[...].reshape(32 * 2 * CAP, BLK)
    summed = exact_dot(hot_ref[...], received)
    out_ref[...] = volume_ref[...] + summed[:32] / jnp.maximum(summed[32:], 1.0)


def on_device(volume, measured, footprint, block_voxel, block_tile, block_rows):
    iota = lambda n: jnp.arange(n, dtype=jnp.int32)
    groups = NB // CAP
    share = block_voxel.reshape(groups, CAP)[:, 0] // 32
    within = block_voxel.reshape(groups, CAP) % 32

    coarse = volume.astype(BF16)
    named = (share[None, :] == iota(32)[:, None]).astype(F32)
    places = jnp.sum(named[:, :, None] * within.astype(F32)[None], axis=1)
    places = jnp.pad(places, ((0, 0), (0, BLK - CAP))).astype(BF16)
    send = jnp.concatenate([jnp.broadcast_to(coarse, (32, 32, BLK)), places[:, None, :]], axis=1)
    slab_values = lax.all_to_all(send, "angle", 0, 0)

    voxel_hot = (block_voxel[:, None] == iota(1024)[None, :]).astype(BF16)
    tile_hot = (block_tile[:, None] == iota(64)[None, :]).astype(BF16)
    tile_hot_t = (block_tile[None, :] == iota(64)[:, None]).astype(BF16)
    live = (iota(BLK)[None, :] < block_rows[:, None]).astype(BF16)

    part = pl.pallas_call(
        forward_kernel,
        out_shape=jax.ShapeDtypeStruct((64, 2 * BLK), F32),
        in_specs=[VMEM] * 5,
        out_specs=VMEM,
        scratch_shapes=[pltpu.VMEM((NB, 2 * BLK), F32)],
        compiler_params=PARAMS,
        name="forward",
    )(slab_values, voxel_hot, tile_hot_t, live, footprint)

    part = part + lax.ppermute(part, "slab", [(i, i ^ 1) for i in range(8)])
    same_core = [[2 * y + c for y in range(4)] for c in range(2)]
    parts = lax.all_to_all(jnp.broadcast_to(part, (4, 64, 2 * BLK)), "slab", 0, 0, axis_index_groups=same_core)

    weighted, send_back = pl.pallas_call(
        backward_kernel,
        out_shape=(
            jax.ShapeDtypeStruct((64, BLK), F32),
            jax.ShapeDtypeStruct((32, 2 * CAP, BLK), F32),
        ),
        in_specs=[SMEM] + [VMEM] * 5,
        out_specs=(VMEM, VMEM),
        scratch_shapes=[pltpu.VMEM((NB, BLK), F32), pltpu.VMEM((2, NB, BLK), F32)],
        compiler_params=PARAMS,
        name="backward",
    )(share, parts, measured, tile_hot, live, footprint)

    received = lax.all_to_all(send_back, "angle", 0, 0)

    place = slab_values[:, 32, :CAP].astype(jnp.int32)
    none = jnp.full_like(place, -1)
    hot_back = jnp.concatenate([place, none], axis=1).reshape(1, -1) == iota(32)[:, None]
    hot_cols = jnp.concatenate([none, place], axis=1).reshape(1, -1) == iota(32)[:, None]
    hot = jnp.concatenate([hot_back, hot_cols], axis=0).astype(BF16)
    new_volume = pl.pallas_call(
        update_kernel,
        out_shape=jax.ShapeDtypeStruct((32, BLK), F32),
        in_specs=[VMEM] * 3,
        out_specs=VMEM,
        compiler_params=PARAMS,
        name="update",
    )(received, hot, volume)
    return new_volume, weighted


def solution(mesh):
    in_specs = (
        P(("slab", "angle"), None),
        P("angle", None),
        P(("slab", "angle"), None, None),
        P(("slab", "angle")),
        P(("slab", "angle")),
        P(("slab", "angle")),
    )
    out_specs = (P(("slab", "angle"), None), P("angle", None))
    return jax.shard_map(
        on_device, mesh=mesh, in_specs=in_specs, out_specs=out_specs, check_vma=False
    )
```

```python
import jax
import jax.numpy as jnp
from jax import lax
from jax.experimental import pallas as pl
from jax.experimental.pallas import tpu as pltpu
from jax.sharding import PartitionSpec as P

BLK = 128
NB = 192
CAP = 12
SHARES = 32
HALF = NB // 2
F32 = jnp.float32
BF16 = jnp.bfloat16
VMEM = pl.BlockSpec(memory_space=pltpu.VMEM)
SMEM = pl.BlockSpec(memory_space=pltpu.SMEM)
HBM = pl.BlockSpec(memory_space=pltpu.HBM)
PARAMS = pltpu.CompilerParams(vmem_limit_bytes=40 * 1024 * 1024)
ROWS = ((1,), (0,))
LANES = ((1,), (1,))
SUBLANES = ((0,), (0,))


def dot(a, b, contract=ROWS):
    return lax.dot_general(a, b, (contract, ((), ())), preferred_element_type=F32)


def iota(shape, dim):
    return lax.broadcasted_iota(jnp.int32, shape, dim)


def exact_dot(onehot, x, contract=ROWS):
    hi = x.astype(BF16)
    rest = x - hi.astype(F32)
    mid = rest.astype(BF16)
    lo = (rest - mid.astype(F32)).astype(BF16)
    return dot(onehot, hi, contract) + (dot(onehot, mid, contract) + dot(onehot, lo, contract))


def offer_kernel(voxel_any, volume_any, foot_any, send_ref, voxel_ref, volume_ref, sems):
    copies = [
        pltpu.make_async_copy(volume_any, volume_ref, sems.at[0]),
        pltpu.make_async_copy(voxel_any, voxel_ref, sems.at[1]),
    ]
    for copy in copies:
        copy.start()
    copies[0].wait()
    coarse = volume_ref[...].astype(BF16)
    for d in range(SHARES):
        send_ref[d, 0:32, :] = coarse
        send_ref[d, 32:40, :] = jnp.zeros((8, BLK), BF16)
    copies[1].wait()
    spot = iota((8, BLK), 0) * BLK + iota((8, BLK), 1) - 2 * CAP * lax.axis_index("angle")
    for j in range(NB // CAP):
        places = jnp.zeros((8, BLK), jnp.int32)
        for i in range(CAP):
            place = (voxel_ref[CAP * j + i] & 31) + 1
            places = jnp.where(spot == i, place, places)
            places = jnp.where(spot == CAP + i, place + 32, places)
        send_ref[voxel_ref[CAP * j] >> 5, 32:40, :] = places.astype(F32).astype(BF16)


def forward_kernel(slab_ref, voxel_ref, tile_ref, rows_ref, foot_ref, part_ref, places_ref):
    places_ref[...] = jnp.sum(slab_ref[:, 32:40, :].astype(F32), axis=0)
    voxel = voxel_ref[...].reshape(1, NB)
    tile = tile_ref[...].reshape(1, NB)
    rows = rows_ref[...].reshape(1, NB)
    voxel_hot = jnp.where(iota((1024, NB), 0) == voxel, 1.0, 0.0).astype(BF16)
    picked = dot(slab_ref[:, 0:32, :].reshape(1024, BLK), voxel_hot, SUBLANES)
    lane = iota((1, BLK), 1)
    even = lane % 2 == 0
    one = jnp.ones((BLK, BLK), F32)
    ones = jnp.concatenate([jnp.where(even, one, 0.0), jnp.where(even, 0.0, one)], axis=0)
    sums = []
    for h in range(2):
        mine = jnp.concatenate([picked[:, HALF * h : HALF * (h + 1)], jnp.zeros((BLK, 32), F32)], axis=1)
        cols = jnp.concatenate([jnp.where(even, mine, 0.0), jnp.where(even, 0.0, mine)], axis=0)
        cols = jnp.concatenate([cols, ones], axis=1).astype(BF16)
        total = jnp.zeros((BLK, 2 * BLK), F32)
        for q in range(HALF // 2):
            k = HALF * h + 2 * q
            pair = jnp.concatenate([foot_ref[k], foot_ref[k + 1]], axis=1)
            both = iota((1, 2 * BLK), 1) % BLK // 2 == q
            total = jnp.where(both, dot(pair, cols), total)
        sums.append(total)
    live = iota((BLK, NB), 0) < rows
    tile_hot = jnp.where(iota((64, NB), 0) == tile, 1.0, 0.0).astype(BF16)
    for n in range(2):
        both = jnp.concatenate([s[:, BLK * n : BLK * n + HALF] for s in sums], axis=1)
        part_ref[:, BLK * n : BLK * (n + 1)] = exact_dot(tile_hot, jnp.where(live, both, 0.0), LANES)


def spread_kernel(mine_ref, other_ref, out_ref):
    both = mine_ref[...] + other_ref[...]
    for y in range(4):
        out_ref[y] = both


def backward_kernel(voxel_ref, parts_ref, measured_ref, tile_ref, rows_ref, foot_ref, weighted_ref, send_ref):
    total = (parts_ref[0] + parts_ref[1]) + (parts_ref[2] + parts_ref[3])
    weighted = (measured_ref[...] - total[:, :BLK]) / jnp.maximum(total[:, BLK:], 1.0)
    weighted_ref[...] = weighted
    tile = tile_ref[...].reshape(1, NB)
    rows = rows_ref[...].reshape(1, NB)
    tile_hot = jnp.where(iota((64, NB), 0) == tile, 1.0, 0.0).astype(BF16)
    live = jnp.where(iota((BLK, NB), 0) < rows, 1.0, 0.0).T
    res = dot(tile_hot, weighted.astype(BF16), SUBLANES) * live
    send_ref[...] = jnp.zeros_like(send_ref)
    row = iota((2 * CAP, BLK), 0) % CAP
    for j in range(NB // CAP):
        at = slice(CAP * j, CAP * (j + 1))
        both = jnp.concatenate([res[at], live[at]], axis=0)
        diag = jnp.concatenate([jnp.where(row == i, both, 0.0) for i in range(CAP)], axis=1).astype(BF16)
        foot = foot_ref[at].reshape(CAP * BLK, BLK)
        send_ref[voxel_ref[CAP * j] >> 5] = dot(diag, foot)


def update_kernel(recv_ref, places_ref, volume_ref, out_ref):
    wanted = (iota((2 * 32, BLK), 0) + 1).astype(F32)
    hot = jnp.concatenate(
        [jnp.where(places_ref[m : m + 1, :] == wanted, 1.0, 0.0) for m in range(SHARES * 2 * CAP // BLK)], axis=1
    ).astype(BF16)
    summed = exact_dot(hot, recv_ref[...].reshape(SHARES * 2 * CAP, BLK))
    out_ref[...] = volume_ref[...] + summed[:32] / jnp.maximum(summed[32:], 1.0)


def call(kernel, name, out, specs, *args):
    out = [jax.ShapeDtypeStruct(*o) for o in out]
    return pl.pallas_call(
        kernel, out_shape=out, in_specs=specs, out_specs=[VMEM] * len(out), compiler_params=PARAMS, name=name
    )(*args)


def on_device(volume, measured, footprint, block_voxel, block_tile, block_rows):
    (offer,) = pl.pallas_call(
        offer_kernel,
        out_shape=[jax.ShapeDtypeStruct((SHARES, 40, BLK), BF16)],
        in_specs=[HBM] * 3,
        out_specs=[VMEM],
        scratch_shapes=[pltpu.SMEM((NB,), jnp.int32), pltpu.VMEM((32, BLK), F32), pltpu.SemaphoreType.DMA((2,))],
        compiler_params=PARAMS,
        name="offer",
    )(*(pltpu.with_memory_space_constraint(x, pltpu.HBM) for x in (block_voxel, volume, footprint)))
    slab_values = lax.all_to_all(offer, "angle", 0, 0)

    part, places = call(
        forward_kernel,
        "forward",
        [((64, 2 * BLK), F32), ((8, BLK), F32)],
        [VMEM] * 5,
        slab_values, block_voxel, block_tile, block_rows, footprint,
    )
    other = lax.ppermute(part, "slab", [(i, i ^ 1) for i in range(8)])
    (spread,) = call(spread_kernel, "spread", [((4, 64, 2 * BLK), F32)], [VMEM] * 2, part, other)
    same_core = [[2 * y + c for y in range(4)] for c in range(2)]
    parts = lax.all_to_all(spread, "slab", 0, 0, axis_index_groups=same_core)

    weighted, send_back = call(
        backward_kernel,
        "backward",
        [((64, BLK), F32), ((SHARES, 2 * CAP, BLK), F32)],
        [SMEM] + [VMEM] * 5,
        block_voxel, parts, measured, block_tile, block_rows, footprint,
    )
    received = lax.all_to_all(send_back, "angle", 0, 0)
    (new_volume,) = call(update_kernel, "update", [((32, BLK), F32)], [VMEM] * 3, received, places, volume)
    return new_volume, weighted


def solution(mesh):
    in_specs = (
        P(("slab", "angle"), None),
        P("angle", None),
        P(("slab", "angle"), None, None),
        P(("slab", "angle")),
        P(("slab", "angle")),
        P(("slab", "angle")),
    )
    out_specs = (P(("slab", "angle"), None), P("angle", None))
    return jax.shard_map(
        on_device, mesh=mesh, in_specs=in_specs, out_specs=out_specs, check_vma=False
    )
```

```python
import jax
import jax.numpy as jnp
from jax import lax
from jax.experimental import pallas as pl
from jax.experimental.pallas import tpu as pltpu
from jax.sharding import PartitionSpec as P

BLK = 128
NB = 192
CAP = 12
SHARES = 32
HALF = NB // 2
F32 = jnp.float32
BF16 = jnp.bfloat16
VMEM = pl.BlockSpec(memory_space=pltpu.VMEM)
SMEM = pl.BlockSpec(memory_space=pltpu.SMEM)
HBM = pl.BlockSpec(memory_space=pltpu.HBM)
PARAMS = pltpu.CompilerParams(vmem_limit_bytes=40 * 1024 * 1024)
ROWS = ((1,), (0,))
LANES = ((1,), (1,))
SUBLANES = ((0,), (0,))


def dot(a, b, contract=ROWS):
    return lax.dot_general(a, b, (contract, ((), ())), preferred_element_type=F32)


def iota(shape, dim):
    return lax.broadcasted_iota(jnp.int32, shape, dim)


def exact_dot(onehot, x, contract=ROWS):
    hi = x.astype(BF16)
    rest = x - hi.astype(F32)
    mid = rest.astype(BF16)
    lo = (rest - mid.astype(F32)).astype(BF16)
    return dot(onehot, hi, contract) + (dot(onehot, mid, contract) + dot(onehot, lo, contract))


def hot_columns(ref, n):
    return jnp.where(iota((n, NB), 0) == ref[...].reshape(1, NB), 1.0, 0.0).astype(BF16)


def live_rows(rows_ref):
    return jnp.where(iota((BLK, NB), 0) < rows_ref[...].reshape(1, NB), 1.0, 0.0).T


def offer_kernel(voxel_any, volume_any, foot_any, send_ref, voxel_ref, volume_ref, sems):
    copies = [
        pltpu.make_async_copy(volume_any, volume_ref, sems.at[0]),
        pltpu.make_async_copy(voxel_any, voxel_ref, sems.at[1]),
    ]
    for copy in copies:
        copy.start()
    copies[0].wait()
    coarse = volume_ref[...].astype(BF16)
    for d in range(SHARES):
        send_ref[d, 0:32, :] = coarse
        send_ref[d, 32:40, :] = jnp.zeros((8, BLK), BF16)
    copies[1].wait()
    spot = iota((8, BLK), 0) * BLK + iota((8, BLK), 1) - 2 * CAP * lax.axis_index("angle")
    for j in range(NB // CAP):
        places = jnp.zeros((8, BLK), jnp.int32)
        for i in range(CAP):
            places = jnp.where(spot == i, (voxel_ref[CAP * j + i] & 31) + 1, places)
        send_ref[voxel_ref[CAP * j] >> 5, 32:40, :] = places.astype(F32).astype(BF16)


def forward_kernel(slab_ref, voxel_ref, tile_ref, rows_ref, foot_ref, part_ref, places_ref):
    picked = dot(slab_ref[:, 0:32, :].reshape(1024, BLK), hot_columns(voxel_ref, 1024), SUBLANES)
    even = iota((1, BLK), 1) % 2 == 0
    one = jnp.ones((BLK, BLK), F32)
    ones = jnp.concatenate([jnp.where(even, one, 0.0), jnp.where(even, 0.0, one)], axis=0)
    sums = []
    for h in range(2):
        mine = jnp.concatenate([picked[:, HALF * h : HALF * (h + 1)], jnp.zeros((BLK, BLK - HALF), F32)], axis=1)
        cols = jnp.concatenate([jnp.where(even, mine, 0.0), jnp.where(even, 0.0, mine)], axis=0)
        cols = jnp.concatenate([cols, ones], axis=1).astype(BF16)
        total = jnp.zeros((BLK, 2 * BLK), F32)
        for q in range(HALF // 2):
            k = HALF * h + 2 * q
            pair = jnp.concatenate([foot_ref[k], foot_ref[k + 1]], axis=1)
            both = iota((1, 2 * BLK), 1) % BLK // 2 == q
            total = jnp.where(both, dot(pair, cols), total)
        sums.append(total)
    live = iota((BLK, NB), 0) < rows_ref[...].reshape(1, NB)
    tile_hot = hot_columns(tile_ref, 64)
    for n in range(2):
        both = jnp.concatenate([x[:, BLK * n : BLK * n + HALF] for x in sums], axis=1)
        part_ref[:, BLK * n : BLK * (n + 1)] = exact_dot(tile_hot, jnp.where(live, both, 0.0), LANES)
    back = jnp.sum(slab_ref[:, 32:40, :].astype(F32), axis=0)
    later = jnp.concatenate([back[:, BLK - CAP :], back[:, : BLK - CAP]], axis=1)
    above = jnp.concatenate([later[7:8], later[:7]], axis=0)
    later = jnp.where(iota((8, BLK), 1) < CAP, above, later)
    places_ref[...] = back + jnp.where(later > 0.0, later + 32.0, 0.0)


def backward_kernel(voxel_ref, mine_ref, across_ref, left_ref, right_ref, measured_ref, tile_ref, rows_ref, foot_ref, weighted_ref, send_ref):
    total = (mine_ref[...] + across_ref[...]) + (left_ref[...] + right_ref[...])
    weighted = (measured_ref[...] - total[:, :BLK]) / jnp.maximum(total[:, BLK:], 1.0)
    weighted_ref[...] = weighted
    live = live_rows(rows_ref)
    residual = dot(hot_columns(tile_ref, 64), weighted.astype(BF16), SUBLANES) * live
    send_ref[...] = jnp.zeros_like(send_ref)
    row = iota((2 * CAP, BLK), 0) % CAP
    for j in range(NB // CAP):
        at = slice(CAP * j, CAP * (j + 1))
        both = jnp.concatenate([residual[at], live[at]], axis=0)
        diag = jnp.concatenate([jnp.where(row == i, both, 0.0) for i in range(CAP)], axis=1).astype(BF16)
        send_ref[voxel_ref[CAP * j] >> 5] = dot(diag, foot_ref[at].reshape(CAP * BLK, BLK))


def update_kernel(recv_ref, places_ref, volume_ref, weighted_ref, out_ref, weighted_out_ref):
    weighted_out_ref[...] = weighted_ref[...]
    wanted = (iota((2 * 32, BLK), 0) + 1).astype(F32)
    hot = jnp.concatenate(
        [jnp.where(places_ref[m : m + 1, :] == wanted, 1.0, 0.0) for m in range(SHARES * 2 * CAP // BLK)], axis=1
    ).astype(BF16)
    summed = exact_dot(hot, recv_ref[...].reshape(SHARES * 2 * CAP, BLK))
    out_ref[...] = volume_ref[...] + summed[:32] / jnp.maximum(summed[32:], 1.0)


def call(kernel, name, out, specs, *args, scratch=()):
    out = [jax.ShapeDtypeStruct(*o) for o in out]
    return pl.pallas_call(
        kernel,
        out_shape=out,
        in_specs=specs,
        out_specs=[VMEM] * len(out),
        scratch_shapes=scratch,
        compiler_params=PARAMS,
        name=name,
    )(*args)


def on_device(volume, measured, footprint, block_voxel, block_tile, block_rows):
    (offer,) = call(
        offer_kernel,
        "offer",
        [((SHARES, 40, BLK), BF16)],
        [HBM] * 3,
        *(pltpu.with_memory_space_constraint(x, pltpu.HBM) for x in (block_voxel, volume, footprint)),
        scratch=[pltpu.SMEM((NB,), jnp.int32), pltpu.VMEM((32, BLK), F32), pltpu.SemaphoreType.DMA((2,))],
    )
    slab_values = lax.all_to_all(offer, "angle", 0, 0)
    part, places = call(
        forward_kernel,
        "forward",
        [((64, 2 * BLK), F32), ((8, BLK), F32)],
        [VMEM] * 5,
        slab_values, block_voxel, block_tile, block_rows, footprint,
    )
    part = part + lax.ppermute(part, "slab", [(i, i ^ 1) for i in range(8)])
    across, left, right = (
        lax.ppermute(part, "slab", [(i, (i + 2 * k) % 8) for i in range(8)]) for k in (2, 1, 3)
    )

    weighted, send_back = call(
        backward_kernel,
        "backward",
        [((64, BLK), F32), ((SHARES, 2 * CAP, BLK), F32)],
        [SMEM] + [VMEM] * 8,
        block_voxel, part, across, left, right, measured, block_tile, block_rows, footprint,
    )
    received = lax.all_to_all(send_back, "angle", 0, 0)
    return call(
        update_kernel,
        "update",
        [((32, BLK), F32), ((64, BLK), F32)],
        [VMEM] * 4,
        received, places, volume, weighted,
    )


def solution(mesh):
    in_specs = (
        P(("slab", "angle"), None),
        P("angle", None),
        P(("slab", "angle"), None, None),
        P(("slab", "angle")),
        P(("slab", "angle")),
        P(("slab", "angle")),
    )
    out_specs = (P(("slab", "angle"), None), P("angle", None))
    return jax.shard_map(
        on_device, mesh=mesh, in_specs=in_specs, out_specs=out_specs, check_vma=False
    )
```

```python
import jax
import jax.numpy as jnp
from jax import lax
from jax.experimental import pallas as pl
from jax.experimental.pallas import tpu as pltpu
from jax.sharding import PartitionSpec as P

BLK = 128
NB = 192
CAP = 12
SHARES = 32
SET = 64
F32 = jnp.float32
BF16 = jnp.bfloat16
VMEM = pl.BlockSpec(memory_space=pltpu.VMEM)
SMEM = pl.BlockSpec(memory_space=pltpu.SMEM)
HBM = pl.BlockSpec(memory_space=pltpu.HBM)
PARAMS = pltpu.CompilerParams(vmem_limit_bytes=40 * 1024 * 1024)
ROWS = ((1,), (0,))
LANES = ((1,), (1,))
SUBLANES = ((0,), (0,))


def dot(a, b, contract=ROWS):
    return lax.dot_general(a, b, (contract, ((), ())), preferred_element_type=F32)


def iota(shape, dim):
    return lax.broadcasted_iota(jnp.int32, shape, dim)


def exact_dot(onehot, x, contract=ROWS):
    hi = x.astype(BF16)
    rest = x - hi.astype(F32)
    mid = rest.astype(BF16)
    lo = (rest - mid.astype(F32)).astype(BF16)
    return dot(onehot, hi, contract) + (dot(onehot, mid, contract) + dot(onehot, lo, contract))


def hot_columns(ref, n):
    return jnp.where(iota((n, NB), 0) == ref[...].reshape(1, NB), 1.0, 0.0).astype(BF16)


def live_rows(rows_ref):
    return jnp.where(iota((BLK, NB), 0) < rows_ref[...].reshape(1, NB), 1.0, 0.0).T


def twice(x):
    return jnp.concatenate([x[:, g : g + SET] for g in range(0, NB, SET) for _ in range(2)], axis=1)


def offer_kernel(voxel_any, volume_any, foot_any, send_ref, voxel_ref, volume_ref, sems):
    copies = [
        pltpu.make_async_copy(volume_any, volume_ref, sems.at[0]),
        pltpu.make_async_copy(voxel_any, voxel_ref, sems.at[1]),
    ]
    for copy in copies:
        copy.start()
    copies[0].wait()
    coarse = volume_ref[...].astype(BF16)
    for d in range(SHARES):
        send_ref[d, 0:32, :] = coarse
        send_ref[d, 32:40, :] = jnp.zeros((8, BLK), BF16)
    copies[1].wait()
    spot = iota((8, BLK), 0) * BLK + iota((8, BLK), 1) - 2 * CAP * lax.axis_index("angle")
    for j in range(NB // CAP):
        places = jnp.zeros((8, BLK), jnp.int32)
        for i in range(CAP):
            places = jnp.where(spot == i, (voxel_ref[CAP * j + i] & 31) + 1, places)
        send_ref[voxel_ref[CAP * j] >> 5, 32:40, :] = places.astype(F32).astype(BF16)


def forward_kernel(slab_ref, voxel_ref, tile_ref, rows_ref, foot_ref, part_ref, places_ref):
    picked = dot(slab_ref[:, 0:32, :].reshape(1024, BLK), hot_columns(voxel_ref, 1024), SUBLANES)
    even = iota((1, BLK), 1) % 2 == 0
    sums = []
    for g in range(0, NB, SET):
        mine = jnp.concatenate([picked[:, g : g + SET], jnp.ones((BLK, SET), F32)], axis=1)
        cols = jnp.concatenate([jnp.where(even, mine, 0.0), jnp.where(even, 0.0, mine)], axis=0).astype(BF16)
        total = jnp.zeros((BLK, BLK), F32)
        for q in range(SET // 2):
            pair = jnp.concatenate([foot_ref[g + 2 * q], foot_ref[g + 2 * q + 1]], axis=1)
            total = jnp.where(iota((1, BLK), 1) % SET // 2 == q, dot(pair, cols), total)
        sums.append(total)
    live = iota((BLK, 2 * NB), 0) < twice(rows_ref[...].reshape(1, NB))
    tile = twice(tile_ref[...].reshape(1, NB))
    wanted = tile + jnp.where(iota((1, 2 * NB), 1) % BLK < SET, 0, 64)
    tile_hot = jnp.where(iota((BLK, 2 * NB), 0) == wanted, 1.0, 0.0).astype(BF16)
    part_ref[...] = exact_dot(tile_hot, jnp.where(live, jnp.concatenate(sums, axis=1), 0.0), LANES)
    back = jnp.sum(slab_ref[:, 32:40, :].astype(F32), axis=0)
    later = jnp.concatenate([back[:, BLK - CAP :], back[:, : BLK - CAP]], axis=1)
    above = jnp.concatenate([later[7:8], later[:7]], axis=0)
    later = jnp.where(iota((8, BLK), 1) < CAP, above, later)
    places_ref[...] = back + jnp.where(later > 0.0, later + 32.0, 0.0)


def backward_kernel(voxel_ref, mine_ref, across_ref, left_ref, right_ref, measured_ref, tile_ref, rows_ref, foot_ref, weighted_ref, send_ref):
    total = (mine_ref[...] + across_ref[...]) + (left_ref[...] + right_ref[...])
    weighted = (measured_ref[...] - total[:64]) / jnp.maximum(total[64:], 1.0)
    weighted_ref[...] = weighted
    live = live_rows(rows_ref)
    residual = dot(hot_columns(tile_ref, 64), weighted.astype(BF16), SUBLANES) * live
    send_ref[...] = jnp.zeros_like(send_ref)
    row = iota((2 * CAP, BLK), 0) % CAP
    for j in range(NB // CAP):
        at = slice(CAP * j, CAP * (j + 1))
        both = jnp.concatenate([residual[at], live[at]], axis=0)
        diag = jnp.concatenate([jnp.where(row == i, both, 0.0) for i in range(CAP)], axis=1).astype(BF16)
        send_ref[voxel_ref[CAP * j] >> 5] = dot(diag, foot_ref[at].reshape(CAP * BLK, BLK))


def update_kernel(recv_ref, places_ref, volume_ref, weighted_ref, out_ref, weighted_out_ref):
    weighted_out_ref[...] = weighted_ref[...]
    wanted = (iota((2 * 32, BLK), 0) + 1).astype(F32)
    hot = jnp.concatenate(
        [jnp.where(places_ref[m : m + 1, :] == wanted, 1.0, 0.0) for m in range(SHARES * 2 * CAP // BLK)], axis=1
    ).astype(BF16)
    summed = exact_dot(hot, recv_ref[...].reshape(SHARES * 2 * CAP, BLK))
    out_ref[...] = volume_ref[...] + summed[:32] / jnp.maximum(summed[32:], 1.0)


def call(kernel, name, out, specs, *args, scratch=()):
    out = [jax.ShapeDtypeStruct(*o) for o in out]
    return pl.pallas_call(
        kernel,
        out_shape=out,
        in_specs=specs,
        out_specs=[VMEM] * len(out),
        scratch_shapes=scratch,
        compiler_params=PARAMS,
        name=name,
    )(*args)


def on_device(volume, measured, footprint, block_voxel, block_tile, block_rows):
    (offer,) = call(
        offer_kernel,
        "offer",
        [((SHARES, 40, BLK), BF16)],
        [HBM] * 3,
        *(pltpu.with_memory_space_constraint(x, pltpu.HBM) for x in (block_voxel, volume, footprint)),
        scratch=[pltpu.SMEM((NB,), jnp.int32), pltpu.VMEM((32, BLK), F32), pltpu.SemaphoreType.DMA((2,))],
    )
    slab_values = lax.all_to_all(offer, "angle", 0, 0)
    part, places = call(
        forward_kernel,
        "forward",
        [((2 * 64, BLK), F32), ((8, BLK), F32)],
        [VMEM] * 5,
        slab_values, block_voxel, block_tile, block_rows, footprint,
    )
    part = part + lax.ppermute(part, "slab", [(i, i ^ 1) for i in range(8)])
    across, left, right = (
        lax.ppermute(part, "slab", [(i, (i + 2 * k) % 8) for i in range(8)]) for k in (2, 1, 3)
    )

    weighted, send_back = call(
        backward_kernel,
        "backward",
        [((64, BLK), F32), ((SHARES, 2 * CAP, BLK), F32)],
        [SMEM] + [VMEM] * 8,
        block_voxel, part, across, left, right, measured, block_tile, block_rows, footprint,
    )
    received = lax.all_to_all(send_back, "angle", 0, 0)
    return call(
        update_kernel,
        "update",
        [((32, BLK), F32), ((64, BLK), F32)],
        [VMEM] * 4,
        received, places, volume, weighted,
    )


def solution(mesh):
    in_specs = (
        P(("slab", "angle"), None),
        P("angle", None),
        P(("slab", "angle"), None, None),
        P(("slab", "angle")),
        P(("slab", "angle")),
        P(("slab", "angle")),
    )
    out_specs = (P(("slab", "angle"), None), P("angle", None))
    return jax.shard_map(
        on_device, mesh=mesh, in_specs=in_specs, out_specs=out_specs, check_vma=False
    )
```

```python
import jax
import jax.numpy as jnp
from jax import lax
from jax.experimental import pallas as pl
from jax.experimental.pallas import tpu as pltpu
from jax.sharding import PartitionSpec as P

BLK = 128
NB = 192
CAP = 12
SHARES = 32
SET = 64
LINES = 2 * CAP
F32 = jnp.float32
BF16 = jnp.bfloat16
VMEM = pl.BlockSpec(memory_space=pltpu.VMEM)
SMEM = pl.BlockSpec(memory_space=pltpu.SMEM)
HBM = pl.BlockSpec(memory_space=pltpu.HBM)
PARAMS = pltpu.CompilerParams(vmem_limit_bytes=40 * 1024 * 1024)
ROWS = ((1,), (0,))
LANES = ((1,), (1,))
SUBLANES = ((0,), (0,))


def dot(a, b, contract=ROWS):
    return lax.dot_general(a, b, (contract, ((), ())), preferred_element_type=F32)


def iota(shape, dim):
    return lax.broadcasted_iota(jnp.int32, shape, dim)


def exact_dot(onehot, x, contract=ROWS):
    hi = x.astype(BF16)
    rest = x - hi.astype(F32)
    mid = rest.astype(BF16)
    lo = (rest - mid.astype(F32)).astype(BF16)
    return dot(onehot, hi, contract) + (dot(onehot, mid, contract) + dot(onehot, lo, contract))


def per_slot(vectors, matrices, group=16):
    row = iota((group, BLK), 0)
    out = []
    for g in range(0, NB, group):
        mine = vectors[g : g + group]
        diag = jnp.concatenate([jnp.where(row == i, mine, 0.0) for i in range(group)], axis=1).astype(BF16)
        out.append(dot(diag, matrices[g : g + group].reshape(group * BLK, BLK)))
    return jnp.concatenate(out, axis=0)


def hot_columns(ref, n):
    return jnp.where(iota((n, NB), 0) == ref[...].reshape(1, NB), 1.0, 0.0).astype(BF16)


def twice(x):
    return jnp.concatenate([x[:, g : g + SET] for g in range(0, NB, SET) for _ in range(2)], axis=1)


def power(k):
    return lax.shift_left(jnp.ones_like(k), k).astype(F32)


def quantize(x, place):
    largest = jnp.max(jnp.abs(x), axis=1, keepdims=True)
    k = jnp.clip(jnp.floor(jnp.log2(jnp.maximum(largest, 2.0**-20))).astype(jnp.int32) + 15, 1, 31)
    q = jnp.clip(jnp.round(x * (power(31 - k) * 0.25)), -32767.0, 32767.0)
    return q.astype(jnp.int32), 128 * (k - 1) + place + 1


def offer_kernel(volume_any, foot_any, send_ref, volume_ref, sem):
    copy = pltpu.make_async_copy(volume_any, volume_ref, sem)
    copy.start()
    copy.wait()
    send_ref[...] = jnp.broadcast_to(volume_ref[...].astype(BF16), (SHARES, 32, BLK))


def forward_kernel(slab_ref, voxel_ref, tile_ref, rows_ref, foot_ref, part_ref):
    picked = dot(slab_ref[...].reshape(1024, BLK), hot_columns(voxel_ref, 1024), SUBLANES)
    even = iota((1, BLK), 1) % 2 == 0
    sums = []
    for g in range(0, NB, SET):
        mine = jnp.concatenate([picked[:, g : g + SET], jnp.ones((BLK, SET), F32)], axis=1)
        cols = jnp.concatenate([jnp.where(even, mine, 0.0), jnp.where(even, 0.0, mine)], axis=0).astype(BF16)
        total = jnp.zeros((BLK, BLK), F32)
        for q in range(SET // 2):
            pair = jnp.concatenate([foot_ref[g + 2 * q], foot_ref[g + 2 * q + 1]], axis=1)
            total = jnp.where(iota((1, BLK), 1) % SET // 2 == q, dot(pair, cols), total)
        sums.append(total)
    live = iota((BLK, 2 * NB), 0) < twice(rows_ref[...].reshape(1, NB))
    tile = twice(tile_ref[...].reshape(1, NB))
    wanted = tile + jnp.where(iota((1, 2 * NB), 1) % BLK < SET, 0, 64)
    tile_hot = jnp.where(iota((BLK, 2 * NB), 0) == wanted, 1.0, 0.0).astype(BF16)
    part_ref[...] = exact_dot(tile_hot, jnp.where(live, jnp.concatenate(sums, axis=1), 0.0), LANES)


def columns_kernel(voxel_ref, rows_ref, foot_ref, live_ref, place_ref, sums_ref, codes_ref):
    live = jnp.where(iota((BLK, NB), 0) < rows_ref[...].reshape(1, NB), 1.0, 0.0).T
    live_ref[...] = live
    place = (jnp.broadcast_to(voxel_ref[...].reshape(1, NB), (BLK, NB)) & 31).astype(F32).T.astype(jnp.int32)
    place_ref[...] = place
    sums_ref[...], codes_ref[...] = quantize(per_slot(live, foot_ref), place + 32)


def backward_kernel(voxel_ref, mine_ref, across_ref, left_ref, right_ref, measured_ref, tile_ref, live_ref, place_ref, sums_ref, codes_ref, foot_ref, weighted_ref, send_ref):
    total = (mine_ref[...] + across_ref[...]) + (left_ref[...] + right_ref[...])
    weighted = (measured_ref[...] - total[:64]) / jnp.maximum(total[64:], 1.0)
    weighted_ref[...] = weighted
    residual = dot(hot_columns(tile_ref, 64), weighted.astype(BF16), SUBLANES) * live_ref[...]
    backs, codes = quantize(per_slot(residual, foot_ref), place_ref[...])
    send_ref[...] = jnp.zeros_like(send_ref)
    first = LINES * lax.axis_index("angle")
    line = iota((LINES, BLK), 0)
    mine = iota((LINES, BLK), 1) == (first + line) & (BLK - 1)
    spot = iota((8, BLK), 0) * BLK + iota((8, BLK), 1) - first
    spot = (spot >= 0) & (spot < LINES)
    for j in range(NB // CAP):
        at = slice(CAP * j, CAP * (j + 1))
        code = jnp.concatenate([codes[at], codes_ref[at]], axis=0)
        code = jnp.sum(jnp.where(mine, code, 0), axis=0, keepdims=True)
        code = jnp.where(spot, jnp.broadcast_to(code, (8, BLK)), 0)
        send_ref[voxel_ref[CAP * j] >> 5] = jnp.concatenate([backs[at], sums_ref[at], code], axis=0).astype(jnp.int16)


def update_kernel(recv_ref, volume_ref, weighted_ref, out_ref, weighted_out_ref):
    weighted_out_ref[...] = weighted_ref[...]
    codes = jnp.sum(recv_ref[:, LINES:, :].astype(jnp.int32), axis=0)
    scale = power(lax.shift_right_logical(codes, 7)) * 2.0**-28
    place = (codes & 127) - 1
    wanted = iota((2 * 32, BLK), 0)
    hot = jnp.concatenate(
        [
            jnp.where(place[m : m + 1, :] == wanted, jnp.broadcast_to(scale[m : m + 1, :], wanted.shape), 0.0)
            for m in range(SHARES * LINES // BLK)
        ],
        axis=1,
    ).astype(BF16)
    values = recv_ref[:, :LINES, :].astype(F32).reshape(SHARES * LINES, BLK)
    high = jnp.floor(values * (1.0 / 256.0)) * 256.0
    summed = dot(hot, high.astype(BF16)) + dot(hot, (values - high).astype(BF16))
    out_ref[...] = volume_ref[...] + summed[:32] / jnp.maximum(summed[32:], 1.0)


def call(kernel, name, out, specs, *args, scratch=()):
    out = [jax.ShapeDtypeStruct(*o) for o in out]
    return pl.pallas_call(
        kernel,
        out_shape=out,
        in_specs=specs,
        out_specs=[VMEM] * len(out),
        scratch_shapes=scratch,
        compiler_params=PARAMS,
        name=name,
    )(*args)


def on_device(volume, measured, footprint, block_voxel, block_tile, block_rows):
    (offer,) = call(
        offer_kernel,
        "offer",
        [((SHARES, 32, BLK), BF16)],
        [HBM] * 2,
        *(pltpu.with_memory_space_constraint(x, pltpu.HBM) for x in (volume, footprint)),
        scratch=[pltpu.VMEM((32, BLK), F32), pltpu.SemaphoreType.DMA],
    )
    slab_values = lax.all_to_all(offer, "angle", 0, 0)
    (part,) = call(
        forward_kernel,
        "forward",
        [((2 * 64, BLK), F32)],
        [VMEM] * 5,
        slab_values, block_voxel, block_tile, block_rows, footprint,
    )
    part = part + lax.ppermute(part, "slab", [(i, i ^ 1) for i in range(8)])
    across, left, right = (
        lax.ppermute(part, "slab", [(i, (i + 2 * k) % 8) for i in range(8)]) for k in (2, 1, 3)
    )
    live, place, column_sums, column_codes = call(
        columns_kernel,
        "columns",
        [((NB, BLK), F32)] + [((NB, BLK), jnp.int32)] * 3,
        [VMEM] * 3,
        block_voxel, block_rows, footprint,
    )
    weighted, send_back = call(
        backward_kernel,
        "backward",
        [((64, BLK), F32), ((SHARES, 32, BLK), jnp.int16)],
        [SMEM] + [VMEM] * 11,
        block_voxel, part, across, left, right, measured, block_tile, live, place, column_sums, column_codes, footprint,
    )
    received = lax.all_to_all(send_back, "angle", 0, 0)
    return call(
        update_kernel,
        "update",
        [((32, BLK), F32), ((64, BLK), F32)],
        [VMEM] * 3,
        received, volume, weighted,
    )


def solution(mesh):
    in_specs = (
        P(("slab", "angle"), None),
        P("angle", None),
        P(("slab", "angle"), None, None),
        P(("slab", "angle")),
        P(("slab", "angle")),
        P(("slab", "angle")),
    )
    out_specs = (P(("slab", "angle"), None), P("angle", None))
    return jax.shard_map(
        on_device, mesh=mesh, in_specs=in_specs, out_specs=out_specs, check_vma=False
    )
```

```python
import jax
import jax.numpy as jnp
from jax import lax
from jax.experimental import pallas as pl
from jax.experimental.pallas import tpu as pltpu
from jax.sharding import PartitionSpec as P

BLK = 128
NB = 192
CAP = 12
SHARES = 32
GROUP = 16
TURNED = 128
SET = NB - TURNED
LINES = 2 * CAP
F32 = jnp.float32
BF16 = jnp.bfloat16
VMEM = pl.BlockSpec(memory_space=pltpu.VMEM)
SMEM = pl.BlockSpec(memory_space=pltpu.SMEM)
HBM = pl.BlockSpec(memory_space=pltpu.HBM)
PARAMS = pltpu.CompilerParams(vmem_limit_bytes=40 * 1024 * 1024)
ROWS = ((1,), (0,))
LANES = ((1,), (1,))
SUBLANES = ((0,), (0,))


def dot(a, b, contract=ROWS):
    return lax.dot_general(a, b, (contract, ((), ())), preferred_element_type=F32)


def iota(shape, dim):
    return lax.broadcasted_iota(jnp.int32, shape, dim)


def exact_dot(onehot, x, contract=ROWS):
    hi = x.astype(BF16)
    rest = x - hi.astype(F32)
    mid = rest.astype(BF16)
    lo = (rest - mid.astype(F32)).astype(BF16)
    return dot(onehot, hi, contract) + (dot(onehot, mid, contract) + dot(onehot, lo, contract))


def per_slot(vectors, matrices, group=GROUP):
    row = iota((group, BLK), 0)
    out = []
    for g in range(0, NB, group):
        mine = vectors[g : g + group]
        diag = jnp.concatenate([jnp.where(row == i, mine, 0.0) for i in range(group)], axis=1).astype(BF16)
        out.append(dot(diag, matrices[g : g + group].reshape(group * BLK, BLK)))
    return jnp.concatenate(out, axis=0)


def hot_columns(ref, n):
    return jnp.where(iota((n, NB), 0) == ref[...].reshape(1, NB), 1.0, 0.0).astype(BF16)


def power(k):
    return lax.shift_left(jnp.ones_like(k), k).astype(F32)


def quantize(x, place):
    largest = jnp.max(jnp.abs(x), axis=1, keepdims=True)
    k = jnp.clip(jnp.floor(jnp.log2(jnp.maximum(largest, 2.0**-20))).astype(jnp.int32) + 15, 1, 31)
    q = jnp.clip(jnp.round(x * (power(31 - k) * 0.25)), -32767.0, 32767.0)
    return q.astype(jnp.int32), 128 * (k - 1) + place + 1


def offer_kernel(volume_any, foot_any, send_ref, volume_ref, sem):
    copy = pltpu.make_async_copy(volume_any, volume_ref, sem)
    copy.start()
    copy.wait()
    send_ref[...] = jnp.broadcast_to(volume_ref[...].astype(BF16), (SHARES, 32, BLK))


def forward_kernel(slab_ref, voxel_ref, tile_ref, rows_ref, foot_ref, part_ref):
    picked = dot(slab_ref[...].reshape(1024, BLK), hot_columns(voxel_ref, 1024), SUBLANES)
    rows = rows_ref[...].reshape(1, NB)
    tile = tile_ref[...].reshape(1, NB)
    twice = lambda x: jnp.concatenate([x[:, TURNED:]] * 2, axis=1)

    lane = iota((1, BLK), 1)
    cols = jnp.concatenate([picked[:, TURNED:], jnp.ones((BLK, SET), F32)], axis=1)
    cols = jnp.concatenate([jnp.where(lane % 2 == n, cols, 0.0) for n in range(2)], axis=0).astype(BF16)
    streamed = jnp.zeros((BLK, BLK), F32)

    values = picked.T
    live = jnp.where(iota((BLK, NB), 0) < rows, 1.0, 0.0).T
    row = iota((GROUP, BLK), 0)
    one = jnp.ones((GROUP, BLK), F32)
    turned = []
    steps = TURNED // GROUP
    for g in range(steps):
        at = slice(GROUP * g, GROUP * (g + 1))
        weights = jnp.concatenate([foot_ref[k].T for k in range(at.start, at.stop)], axis=0)
        for q in range(SET // 2 * g // steps, SET // 2 * (g + 1) // steps):
            k = TURNED + 2 * q
            pair = jnp.concatenate([foot_ref[k], foot_ref[k + 1]], axis=1)
            streamed = jnp.where(lane % SET // 2 == q, dot(pair, cols), streamed)
        both = jnp.concatenate([values[at], one], axis=0)
        both_row = jnp.concatenate([row, row], axis=0)
        diag = jnp.concatenate([jnp.where(both_row == i, both, 0.0) for i in range(GROUP)], axis=1)
        out = dot(diag.astype(BF16), weights)
        turned.append(jnp.concatenate([out[:GROUP] * live[at], out[GROUP:] * live[at]], axis=1))
    tile_hot = jnp.where(iota((64, TURNED), 0) == tile[:, :TURNED], 1.0, 0.0).astype(BF16)
    first = exact_dot(tile_hot, jnp.concatenate(turned, axis=0))
    wanted = twice(tile) + jnp.where(lane < SET, 0, 64)
    tile_hot = jnp.where(iota((BLK, BLK), 0) == wanted, 1.0, 0.0).astype(BF16)
    second = exact_dot(tile_hot, jnp.where(iota((BLK, BLK), 0) < twice(rows), streamed, 0.0), LANES)
    part_ref[...] = jnp.concatenate([first[:, :BLK], first[:, BLK:]], axis=0) + second


def columns_kernel(voxel_ref, rows_ref, foot_ref, live_ref, place_ref, sums_ref, codes_ref):
    live = jnp.where(iota((BLK, NB), 0) < rows_ref[...].reshape(1, NB), 1.0, 0.0).T
    live_ref[...] = live
    place = (jnp.broadcast_to(voxel_ref[...].reshape(1, NB), (BLK, NB)) & 31).astype(F32).T.astype(jnp.int32)
    place_ref[...] = place
    sums_ref[...], codes_ref[...] = quantize(per_slot(live, foot_ref), place + 32)


def backward_kernel(voxel_ref, mine_ref, across_ref, left_ref, right_ref, measured_ref, tile_ref, live_ref, place_ref, sums_ref, codes_ref, foot_ref, weighted_ref, send_ref):
    total = (mine_ref[...] + across_ref[...]) + (left_ref[...] + right_ref[...])
    weighted = (measured_ref[...] - total[:64]) / jnp.maximum(total[64:], 1.0)
    weighted_ref[...] = weighted
    residual = dot(hot_columns(tile_ref, 64), weighted.astype(BF16), SUBLANES) * live_ref[...]
    backs, codes = quantize(per_slot(residual, foot_ref), place_ref[...])
    send_ref[...] = jnp.zeros_like(send_ref)
    first = LINES * lax.axis_index("angle")
    line = iota((LINES, BLK), 0)
    mine = iota((LINES, BLK), 1) == (first + line) & (BLK - 1)
    spot = iota((8, BLK), 0) * BLK + iota((8, BLK), 1) - first
    spot = (spot >= 0) & (spot < LINES)
    for j in range(NB // CAP):
        at = slice(CAP * j, CAP * (j + 1))
        code = jnp.concatenate([codes[at], codes_ref[at]], axis=0)
        code = jnp.sum(jnp.where(mine, code, 0), axis=0, keepdims=True)
        code = jnp.where(spot, jnp.broadcast_to(code, (8, BLK)), 0)
        send_ref[voxel_ref[CAP * j] >> 5] = jnp.concatenate([backs[at], sums_ref[at], code], axis=0).astype(jnp.int16)


def update_kernel(recv_ref, volume_ref, weighted_ref, out_ref, weighted_out_ref):
    weighted_out_ref[...] = weighted_ref[...]
    codes = jnp.sum(recv_ref[:, LINES:, :].astype(jnp.int32), axis=0)
    scale = power(lax.shift_right_logical(codes, 7)) * 2.0**-28
    place = (codes & 127) - 1
    wanted = iota((2 * 32, BLK), 0)
    hot = jnp.concatenate(
        [
            jnp.where(place[m : m + 1, :] == wanted, jnp.broadcast_to(scale[m : m + 1, :], wanted.shape), 0.0)
            for m in range(SHARES * LINES // BLK)
        ],
        axis=1,
    ).astype(BF16)
    values = recv_ref[:, :LINES, :].astype(F32).reshape(SHARES * LINES, BLK)
    high = jnp.floor(values * (1.0 / 256.0)) * 256.0
    summed = dot(hot, high.astype(BF16)) + dot(hot, (values - high).astype(BF16))
    out_ref[...] = volume_ref[...] + summed[:32] / jnp.maximum(summed[32:], 1.0)


def call(kernel, name, out, specs, *args, scratch=()):
    out = [jax.ShapeDtypeStruct(*o) for o in out]
    return pl.pallas_call(
        kernel,
        out_shape=out,
        in_specs=specs,
        out_specs=[VMEM] * len(out),
        scratch_shapes=scratch,
        compiler_params=PARAMS,
        name=name,
    )(*args)


def on_device(volume, measured, footprint, block_voxel, block_tile, block_rows):
    (offer,) = call(
        offer_kernel,
        "offer",
        [((SHARES, 32, BLK), BF16)],
        [HBM] * 2,
        *(pltpu.with_memory_space_constraint(x, pltpu.HBM) for x in (volume, footprint)),
        scratch=[pltpu.VMEM((32, BLK), F32), pltpu.SemaphoreType.DMA],
    )
    slab_values = lax.all_to_all(offer, "angle", 0, 0)
    (part,) = call(
        forward_kernel,
        "forward",
        [((2 * 64, BLK), F32)],
        [VMEM] * 5,
        slab_values, block_voxel, block_tile, block_rows, footprint,
    )
    part = part + lax.ppermute(part, "slab", [(i, i ^ 1) for i in range(8)])
    across, left, right = (
        lax.ppermute(part, "slab", [(i, (i + 2 * k) % 8) for i in range(8)]) for k in (2, 1, 3)
    )
    live, place, column_sums, column_codes = call(
        columns_kernel,
        "columns",
        [((NB, BLK), F32)] + [((NB, BLK), jnp.int32)] * 3,
        [VMEM] * 3,
        block_voxel, block_rows, footprint,
    )
    weighted, send_back = call(
        backward_kernel,
        "backward",
        [((64, BLK), F32), ((SHARES, 32, BLK), jnp.int16)],
        [SMEM] + [VMEM] * 11,
        block_voxel, part, across, left, right, measured, block_tile, live, place, column_sums, column_codes, footprint,
    )
    received = lax.all_to_all(send_back, "angle", 0, 0)
    return call(
        update_kernel,
        "update",
        [((32, BLK), F32), ((64, BLK), F32)],
        [VMEM] * 3,
        received, volume, weighted,
    )


def solution(mesh):
    in_specs = (
        P(("slab", "angle"), None),
        P("angle", None),
        P(("slab", "angle"), None, None),
        P(("slab", "angle")),
        P(("slab", "angle")),
        P(("slab", "angle")),
    )
    out_specs = (P(("slab", "angle"), None), P("angle", None))
    return jax.shard_map(
        on_device, mesh=mesh, in_specs=in_specs, out_specs=out_specs, check_vma=False
    )
```

```python
import jax
import jax.numpy as jnp
from jax import lax
from jax.experimental import pallas as pl
from jax.experimental.pallas import tpu as pltpu
from jax.sharding import PartitionSpec as P

BLK = 128
NB = 192
CAP = 12
SHARES = 32
GROUP = 16
TURNED = 128
SET = NB - TURNED
LINES = 2 * CAP
F32 = jnp.float32
BF16 = jnp.bfloat16
VMEM = pl.BlockSpec(memory_space=pltpu.VMEM)
HBM = pl.BlockSpec(memory_space=pltpu.HBM)
PARAMS = pltpu.CompilerParams(vmem_limit_bytes=40 * 1024 * 1024)
ROWS = ((1,), (0,))
LANES = ((1,), (1,))
SUBLANES = ((0,), (0,))


def dot(a, b, contract=ROWS):
    return lax.dot_general(a, b, (contract, ((), ())), preferred_element_type=F32)


def iota(shape, dim):
    return lax.broadcasted_iota(jnp.int32, shape, dim)


def exact_dot(onehot, x, contract=ROWS):
    hi = x.astype(BF16)
    rest = x - hi.astype(F32)
    mid = rest.astype(BF16)
    lo = (rest - mid.astype(F32)).astype(BF16)
    return dot(onehot, hi, contract) + (dot(onehot, mid, contract) + dot(onehot, lo, contract))


def per_slot(vectors, matrices, group=GROUP):
    row = iota((group, BLK), 0)
    out = []
    for g in range(0, NB, group):
        mine = vectors[g : g + group]
        diag = jnp.concatenate([jnp.where(row == i, mine, 0.0) for i in range(group)], axis=1).astype(BF16)
        out.append(dot(diag, matrices[g : g + group].reshape(group * BLK, BLK)))
    return jnp.concatenate(out, axis=0)


def hot_columns(ref, n):
    return jnp.where(iota((n, NB), 0) == ref[...].reshape(1, NB), 1.0, 0.0).astype(BF16)


def power(k):
    return lax.shift_left(jnp.ones_like(k), k).astype(F32)


def quantize(x, place):
    largest = jnp.max(jnp.abs(x), axis=1, keepdims=True)
    k = jnp.clip(jnp.floor(jnp.log2(jnp.maximum(largest, 2.0**-20))).astype(jnp.int32) + 15, 1, 31)
    q = jnp.clip(jnp.round(x * (power(31 - k) * 0.25)), -32767.0, 32767.0)
    return q.astype(jnp.int32), 128 * (k - 1) + place + 1


def offer_kernel(volume_any, foot_any, send_ref, volume_ref, sem):
    copy = pltpu.make_async_copy(volume_any, volume_ref, sem)
    copy.start()
    copy.wait()
    send_ref[...] = jnp.broadcast_to(volume_ref[...].astype(BF16), (SHARES, 32, BLK))


def forward_kernel(slab_ref, voxel_ref, tile_ref, rows_ref, foot_ref, part_ref):
    picked = dot(slab_ref[...].reshape(1024, BLK), hot_columns(voxel_ref, 1024), SUBLANES)
    rows = rows_ref[...].reshape(1, NB)
    tile = tile_ref[...].reshape(1, NB)
    twice = lambda x: jnp.concatenate([x[:, TURNED:]] * 2, axis=1)

    lane = iota((1, BLK), 1)
    cols = jnp.concatenate([picked[:, TURNED:], jnp.ones((BLK, SET), F32)], axis=1)
    cols = jnp.concatenate([jnp.where(lane % 2 == n, cols, 0.0) for n in range(2)], axis=0).astype(BF16)
    streamed = jnp.zeros((BLK, BLK), F32)

    values = picked.T
    live = jnp.where(iota((BLK, NB), 0) < rows, 1.0, 0.0).T
    row = iota((GROUP, BLK), 0)
    one = jnp.ones((GROUP, BLK), F32)
    turned = []
    steps = TURNED // GROUP
    for g in range(steps):
        at = slice(GROUP * g, GROUP * (g + 1))
        weights = jnp.concatenate([foot_ref[k].T for k in range(at.start, at.stop)], axis=0)
        for q in range(SET // 2 * g // steps, SET // 2 * (g + 1) // steps):
            k = TURNED + 2 * q
            pair = jnp.concatenate([foot_ref[k], foot_ref[k + 1]], axis=1)
            streamed = jnp.where(lane % SET // 2 == q, dot(pair, cols), streamed)
        both = jnp.concatenate([values[at], one], axis=0)
        both_row = jnp.concatenate([row, row], axis=0)
        diag = jnp.concatenate([jnp.where(both_row == i, both, 0.0) for i in range(GROUP)], axis=1)
        out = dot(diag.astype(BF16), weights)
        turned.append(jnp.concatenate([out[:GROUP] * live[at], out[GROUP:] * live[at]], axis=1))
    tile_hot = jnp.where(iota((64, TURNED), 0) == tile[:, :TURNED], 1.0, 0.0).astype(BF16)
    first = exact_dot(tile_hot, jnp.concatenate(turned, axis=0))
    wanted = twice(tile) + jnp.where(lane < SET, 0, 64)
    tile_hot = jnp.where(iota((BLK, BLK), 0) == wanted, 1.0, 0.0).astype(BF16)
    second = exact_dot(tile_hot, jnp.where(iota((BLK, BLK), 0) < twice(rows), streamed, 0.0), LANES)
    part_ref[...] = jnp.concatenate([first[:, :BLK], first[:, BLK:]], axis=0) + second


def columns_kernel(voxel_ref, rows_ref, foot_ref, live_ref, place_ref, sums_ref, codes_ref):
    live = jnp.where(iota((BLK, NB), 0) < rows_ref[...].reshape(1, NB), 1.0, 0.0).T
    live_ref[...] = live
    place = (jnp.broadcast_to(voxel_ref[...].reshape(1, NB), (BLK, NB)) & 31).astype(F32).T.astype(jnp.int32)
    place_ref[...] = place
    sums_ref[...], codes_ref[...] = quantize(per_slot(live, foot_ref), place + 32)


def backward_kernel(voxel_any, mine_ref, across_ref, left_ref, right_ref, measured_ref, tile_ref, live_ref, place_ref, sums_ref, codes_ref, foot_ref, weighted_ref, send_ref, voxel_ref, sem):
    voxel_copy = pltpu.make_async_copy(voxel_any, voxel_ref, sem)
    voxel_copy.start()
    total = (mine_ref[...] + across_ref[...]) + (left_ref[...] + right_ref[...])
    weighted = (measured_ref[...] - total[:64]) / jnp.maximum(total[64:], 1.0)
    weighted_ref[...] = weighted
    residual = dot(hot_columns(tile_ref, 64), weighted.astype(BF16), SUBLANES) * live_ref[...]
    backs, codes = quantize(per_slot(residual, foot_ref), place_ref[...])
    send_ref[...] = jnp.zeros_like(send_ref)
    first = LINES * lax.axis_index("angle")
    line = iota((LINES, BLK), 0)
    mine = iota((LINES, BLK), 1) == (first + line) & (BLK - 1)
    spot = iota((8, BLK), 0) * BLK + iota((8, BLK), 1) - first
    spot = (spot >= 0) & (spot < LINES)
    voxel_copy.wait()
    for j in range(NB // CAP):
        at = slice(CAP * j, CAP * (j + 1))
        code = jnp.concatenate([codes[at], codes_ref[at]], axis=0)
        code = jnp.sum(jnp.where(mine, code, 0), axis=0, keepdims=True)
        code = jnp.where(spot, jnp.broadcast_to(code, (8, BLK)), 0)
        send_ref[voxel_ref[CAP * j] >> 5] = jnp.concatenate([backs[at], sums_ref[at], code], axis=0).astype(jnp.int16)


def update_kernel(recv_ref, volume_ref, weighted_ref, out_ref, weighted_out_ref):
    weighted_out_ref[...] = weighted_ref[...]
    codes = jnp.sum(recv_ref[:, LINES:, :].astype(jnp.int32), axis=0)
    scale = power(lax.shift_right_logical(codes, 7)) * 2.0**-28
    place = (codes & 127) - 1
    wanted = iota((2 * 32, BLK), 0)
    hot = jnp.concatenate(
        [
            jnp.where(place[m : m + 1, :] == wanted, jnp.broadcast_to(scale[m : m + 1, :], wanted.shape), 0.0)
            for m in range(SHARES * LINES // BLK)
        ],
        axis=1,
    ).astype(BF16)
    values = recv_ref[:, :LINES, :].astype(F32).reshape(SHARES * LINES, BLK)
    high = jnp.floor(values * (1.0 / 256.0)) * 256.0
    summed = dot(hot, high.astype(BF16)) + dot(hot, (values - high).astype(BF16))
    out_ref[...] = volume_ref[...] + summed[:32] / jnp.maximum(summed[32:], 1.0)


def call(kernel, name, out, specs, *args, scratch=()):
    out = [jax.ShapeDtypeStruct(*o) for o in out]
    return pl.pallas_call(
        kernel,
        out_shape=out,
        in_specs=specs,
        out_specs=[VMEM] * len(out),
        scratch_shapes=scratch,
        compiler_params=PARAMS,
        name=name,
    )(*args)


def on_device(volume, measured, footprint, block_voxel, block_tile, block_rows):
    (offer,) = call(
        offer_kernel,
        "offer",
        [((SHARES, 32, BLK), BF16)],
        [HBM] * 2,
        *(pltpu.with_memory_space_constraint(x, pltpu.HBM) for x in (volume, footprint)),
        scratch=[pltpu.VMEM((32, BLK), F32), pltpu.SemaphoreType.DMA],
    )
    slab_values = lax.all_to_all(offer, "angle", 0, 0)
    (part,) = call(
        forward_kernel,
        "forward",
        [((2 * 64, BLK), F32)],
        [VMEM] * 5,
        slab_values, block_voxel, block_tile, block_rows, footprint,
    )
    part = part + lax.ppermute(part, "slab", [(i, i ^ 1) for i in range(8)])
    across, left, right = (
        lax.ppermute(part, "slab", [(i, (i + 2 * k) % 8) for i in range(8)]) for k in (2, 1, 3)
    )
    live, place, column_sums, column_codes = call(
        columns_kernel,
        "columns",
        [((NB, BLK), F32)] + [((NB, BLK), jnp.int32)] * 3,
        [VMEM] * 3,
        block_voxel, block_rows, footprint,
    )
    weighted, send_back = call(
        backward_kernel,
        "backward",
        [((64, BLK), F32), ((SHARES, 32, BLK), jnp.int16)],
        [VMEM] * 12,
        block_voxel, part, across, left, right, measured, block_tile, live, place, column_sums, column_codes, footprint,
        scratch=[pltpu.SMEM((NB,), jnp.int32), pltpu.SemaphoreType.DMA],
    )
    received = lax.all_to_all(send_back, "angle", 0, 0)
    return call(
        update_kernel,
        "update",
        [((32, BLK), F32), ((64, BLK), F32)],
        [VMEM] * 3,
        received, volume, weighted,
    )


def solution(mesh):
    in_specs = (
        P(("slab", "angle"), None),
        P("angle", None),
        P(("slab", "angle"), None, None),
        P(("slab", "angle")),
        P(("slab", "angle")),
        P(("slab", "angle")),
    )
    out_specs = (P(("slab", "angle"), None), P("angle", None))
    return jax.shard_map(
        on_device, mesh=mesh, in_specs=in_specs, out_specs=out_specs, check_vma=False
    )
```

```python
import jax
import jax.numpy as jnp
from jax import lax
from jax.experimental import pallas as pl
from jax.experimental.pallas import tpu as pltpu
from jax.sharding import PartitionSpec as P

BLK = 128
NB = 192
CAP = 12
SHARES = 32
GROUP = 16
TURNED = 128
SET = NB - TURNED
LINES = 2 * CAP
F32 = jnp.float32
BF16 = jnp.bfloat16
VMEM = pl.BlockSpec(memory_space=pltpu.VMEM)
HBM = pl.BlockSpec(memory_space=pltpu.HBM)
PARAMS = pltpu.CompilerParams(vmem_limit_bytes=40 * 1024 * 1024)
ROWS = ((1,), (0,))
LANES = ((1,), (1,))
SUBLANES = ((0,), (0,))


def dot(a, b, contract=ROWS):
    return lax.dot_general(a, b, (contract, ((), ())), preferred_element_type=F32)


def iota(shape, dim):
    return lax.broadcasted_iota(jnp.int32, shape, dim)


def exact_dot(onehot, x, contract=ROWS):
    hi = x.astype(BF16)
    rest = x - hi.astype(F32)
    mid = rest.astype(BF16)
    lo = (rest - mid.astype(F32)).astype(BF16)
    return dot(onehot, hi, contract) + (dot(onehot, mid, contract) + dot(onehot, lo, contract))


def per_slot(vectors, matrices, group=GROUP):
    row = iota((group, BLK), 0)
    out = []
    for g in range(0, NB, group):
        mine = vectors[g : g + group]
        diag = jnp.concatenate([jnp.where(row == i, mine, 0.0) for i in range(group)], axis=1).astype(BF16)
        out.append(dot(diag, matrices[g : g + group].reshape(group * BLK, BLK)))
    return jnp.concatenate(out, axis=0)


def hot_columns(ref, n):
    return jnp.where(iota((n, NB), 0) == ref[...].reshape(1, NB), 1.0, 0.0).astype(BF16)


def power(k):
    return lax.shift_left(jnp.ones_like(k), k).astype(F32)


def quantize(x, place):
    largest = jnp.max(jnp.abs(x), axis=1, keepdims=True)
    k = jnp.clip(jnp.floor(jnp.log2(jnp.maximum(largest, 2.0**-20))).astype(jnp.int32) + 15, 1, 31)
    q = jnp.clip(jnp.round(x * (power(31 - k) * 0.25)), -32767.0, 32767.0)
    return q.astype(jnp.int32), 128 * (k - 1) + place + 1


def offer_kernel(volume_any, foot_any, send_ref, volume_ref, sem):
    copy = pltpu.make_async_copy(volume_any, volume_ref, sem)
    copy.start()
    copy.wait()
    send_ref[...] = jnp.broadcast_to(volume_ref[...].astype(BF16), (SHARES, 32, BLK))


def forward_kernel(slab_ref, voxel_ref, tile_ref, rows_ref, foot_ref, part_ref):
    picked = dot(slab_ref[...].reshape(1024, BLK), hot_columns(voxel_ref, 1024), SUBLANES)
    rows = rows_ref[...].reshape(1, NB)
    tile = tile_ref[...].reshape(1, NB)
    twice = lambda x: jnp.concatenate([x[:, TURNED:]] * 2, axis=1)

    lane = iota((1, BLK), 1)
    cols = jnp.concatenate([picked[:, TURNED:], jnp.ones((BLK, SET), F32)], axis=1)
    cols = jnp.concatenate([jnp.where(lane % 2 == n, cols, 0.0) for n in range(2)], axis=0).astype(BF16)
    streamed = jnp.zeros((BLK, BLK), F32)

    values = picked.T
    live = jnp.where(iota((BLK, NB), 0) < rows, 1.0, 0.0).T
    row = iota((GROUP, BLK), 0)
    one = jnp.ones((GROUP, BLK), F32)
    turned = []
    steps = TURNED // GROUP
    for g in range(steps):
        at = slice(GROUP * g, GROUP * (g + 1))
        weights = jnp.concatenate([foot_ref[k].T for k in range(at.start, at.stop)], axis=0)
        for q in range(SET // 2 * g // steps, SET // 2 * (g + 1) // steps):
            k = TURNED + 2 * q
            pair = jnp.concatenate([foot_ref[k], foot_ref[k + 1]], axis=1)
            streamed = jnp.where(lane % SET // 2 == q, dot(pair, cols), streamed)
        both = jnp.concatenate([values[at], one], axis=0)
        both_row = jnp.concatenate([row, row], axis=0)
        diag = jnp.concatenate([jnp.where(both_row == i, both, 0.0) for i in range(GROUP)], axis=1)
        out = dot(diag.astype(BF16), weights)
        turned.append(jnp.concatenate([out[:GROUP] * live[at], out[GROUP:] * live[at]], axis=1))
    tile_hot = jnp.where(iota((64, TURNED), 0) == tile[:, :TURNED], 1.0, 0.0).astype(BF16)
    first = exact_dot(tile_hot, jnp.concatenate(turned, axis=0))
    wanted = twice(tile) + jnp.where(lane < SET, 0, 64)
    tile_hot = jnp.where(iota((BLK, BLK), 0) == wanted, 1.0, 0.0).astype(BF16)
    second = exact_dot(tile_hot, jnp.where(iota((BLK, BLK), 0) < twice(rows), streamed, 0.0), LANES)
    part_ref[...] = jnp.concatenate([first[:, :BLK], first[:, BLK:]], axis=0) + second


def columns_kernel(voxel_ref, rows_ref, foot_ref, live_ref, place_ref, sums_ref, codes_ref):
    live = jnp.where(iota((BLK, NB), 0) < rows_ref[...].reshape(1, NB), 1.0, 0.0).T
    live_ref[...] = live
    place = (jnp.broadcast_to(voxel_ref[...].reshape(1, NB), (BLK, NB)) & 31).astype(F32).T.astype(jnp.int32)
    place_ref[...] = place
    sums_ref[...], codes_ref[...] = quantize(per_slot(live, foot_ref), place + 32)


def backward_kernel(voxel_any, mine_ref, right_ref, left_ref, across_ref, measured_ref, tile_ref, live_ref, place_ref, sums_ref, codes_ref, foot_ref, weighted_ref, send_ref, voxel_ref, sem):
    voxel_copy = pltpu.make_async_copy(voxel_any, voxel_ref, sem)
    voxel_copy.start()
    total = (mine_ref[...] + across_ref[...]) + (left_ref[...] + right_ref[...])
    weighted = (measured_ref[...] - total[:64]) / jnp.maximum(total[64:], 1.0)
    weighted_ref[...] = weighted
    residual = dot(hot_columns(tile_ref, 64), weighted.astype(BF16), SUBLANES) * live_ref[...]
    backs, codes = quantize(per_slot(residual, foot_ref), place_ref[...])
    send_ref[...] = jnp.zeros_like(send_ref)
    first = LINES * lax.axis_index("angle")
    line = iota((LINES, BLK), 0)
    mine = iota((LINES, BLK), 1) == (first + line) & (BLK - 1)
    spot = iota((8, BLK), 0) * BLK + iota((8, BLK), 1) - first
    spot = (spot >= 0) & (spot < LINES)
    voxel_copy.wait()
    for j in range(NB // CAP):
        at = slice(CAP * j, CAP * (j + 1))
        code = jnp.concatenate([codes[at], codes_ref[at]], axis=0)
        code = jnp.sum(jnp.where(mine, code, 0), axis=0, keepdims=True)
        code = jnp.where(spot, jnp.broadcast_to(code, (8, BLK)), 0)
        send_ref[voxel_ref[CAP * j] >> 5] = jnp.concatenate([backs[at], sums_ref[at], code], axis=0).astype(jnp.int16)


def update_kernel(recv_ref, volume_ref, weighted_ref, out_ref, weighted_out_ref):
    weighted_out_ref[...] = weighted_ref[...]
    codes = jnp.sum(recv_ref[:, LINES:, :].astype(jnp.int32), axis=0)
    scale = power(lax.shift_right_logical(codes, 7)) * 2.0**-28
    place = (codes & 127) - 1
    wanted = iota((2 * 32, BLK), 0)
    hot = jnp.concatenate(
        [
            jnp.where(place[m : m + 1, :] == wanted, jnp.broadcast_to(scale[m : m + 1, :], wanted.shape), 0.0)
            for m in range(SHARES * LINES // BLK)
        ],
        axis=1,
    ).astype(BF16)
    values = recv_ref[:, :LINES, :].astype(F32).reshape(SHARES * LINES, BLK)
    high = jnp.floor(values * (1.0 / 256.0)) * 256.0
    summed = dot(hot, high.astype(BF16)) + dot(hot, (values - high).astype(BF16))
    out_ref[...] = volume_ref[...] + summed[:32] / jnp.maximum(summed[32:], 1.0)


def call(kernel, name, out, specs, *args, scratch=()):
    out = [jax.ShapeDtypeStruct(*o) for o in out]
    return pl.pallas_call(
        kernel,
        out_shape=out,
        in_specs=specs,
        out_specs=[VMEM] * len(out),
        scratch_shapes=scratch,
        compiler_params=PARAMS,
        name=name,
    )(*args)


def on_device(volume, measured, footprint, block_voxel, block_tile, block_rows):
    (offer,) = call(
        offer_kernel,
        "offer",
        [((SHARES, 32, BLK), BF16)],
        [HBM] * 2,
        *(pltpu.with_memory_space_constraint(x, pltpu.HBM) for x in (volume, footprint)),
        scratch=[pltpu.VMEM((32, BLK), F32), pltpu.SemaphoreType.DMA],
    )
    slab_values = lax.all_to_all(offer, "angle", 0, 0)
    (part,) = call(
        forward_kernel,
        "forward",
        [((2 * 64, BLK), F32)],
        [VMEM] * 5,
        slab_values, block_voxel, block_tile, block_rows, footprint,
    )
    part = part + lax.ppermute(part, "slab", [(i, i ^ 1) for i in range(8)])
    left = lax.ppermute(part, "slab", [(i, i ^ 2) for i in range(8)])
    right = lax.ppermute(part, "slab", [(i, 6 - i + 2 * (i % 2)) for i in range(8)])
    across = lax.ppermute(part, "slab", [(i, i ^ 4) for i in range(8)])
    live, place, column_sums, column_codes = call(
        columns_kernel,
        "columns",
        [((NB, BLK), F32)] + [((NB, BLK), jnp.int32)] * 3,
        [VMEM] * 3,
        block_voxel, block_rows, footprint,
    )
    weighted, send_back = call(
        backward_kernel,
        "backward",
        [((64, BLK), F32), ((SHARES, 32, BLK), jnp.int16)],
        [VMEM] * 12,
        block_voxel, part, right, left, across, measured, block_tile, live, place, column_sums, column_codes, footprint,
        scratch=[pltpu.SMEM((NB,), jnp.int32), pltpu.SemaphoreType.DMA],
    )
    received = lax.all_to_all(send_back, "angle", 0, 0)
    return call(
        update_kernel,
        "update",
        [((32, BLK), F32), ((64, BLK), F32)],
        [VMEM] * 3,
        received, volume, weighted,
    )


def solution(mesh):
    in_specs = (
        P(("slab", "angle"), None),
        P("angle", None),
        P(("slab", "angle"), None, None),
        P(("slab", "angle")),
        P(("slab", "angle")),
        P(("slab", "angle")),
    )
    out_specs = (P(("slab", "angle"), None), P("angle", None))
    return jax.shard_map(
        on_device, mesh=mesh, in_specs=in_specs, out_specs=out_specs, check_vma=False
    )
```

```python
import jax
import jax.numpy as jnp
from jax import lax
from jax.experimental import pallas as pl
from jax.experimental.pallas import tpu as pltpu
from jax.sharding import PartitionSpec as P

BLK = 128
NB = 192
CAP = 12
SHARES = 32
GROUP = 16
TURNED = 128
SET = NB - TURNED
LINES = 2 * CAP
F32 = jnp.float32
BF16 = jnp.bfloat16
VMEM = pl.BlockSpec(memory_space=pltpu.VMEM)
HBM = pl.BlockSpec(memory_space=pltpu.HBM)
PARAMS = pltpu.CompilerParams(vmem_limit_bytes=40 * 1024 * 1024)
ROWS = ((1,), (0,))
LANES = ((1,), (1,))
SUBLANES = ((0,), (0,))


def dot(a, b, contract=ROWS):
    return lax.dot_general(a, b, (contract, ((), ())), preferred_element_type=F32)


def iota(shape, dim):
    return lax.broadcasted_iota(jnp.int32, shape, dim)


def exact_dot(onehot, x, contract=ROWS):
    hi = x.astype(BF16)
    rest = x - hi.astype(F32)
    mid = rest.astype(BF16)
    lo = (rest - mid.astype(F32)).astype(BF16)
    return dot(onehot, hi, contract) + (dot(onehot, mid, contract) + dot(onehot, lo, contract))


def per_slot(vectors, matrices, group=GROUP):
    row = iota((group, BLK), 0)
    out = []
    for g in range(0, NB, group):
        mine = vectors[g : g + group]
        diag = jnp.concatenate([jnp.where(row == i, mine, 0.0) for i in range(group)], axis=1).astype(BF16)
        out.append(dot(diag, matrices[g : g + group].reshape(group * BLK, BLK)))
    return jnp.concatenate(out, axis=0)


def hot_columns(ref, n):
    return jnp.where(iota((n, NB), 0) == ref[...].reshape(1, NB), 1.0, 0.0).astype(BF16)


def power(k):
    return lax.shift_left(jnp.ones_like(k), k).astype(F32)


def quantize(x, place):
    largest = jnp.max(jnp.abs(x), axis=1, keepdims=True)
    k = jnp.clip(jnp.floor(jnp.log2(jnp.maximum(largest, 2.0**-20))).astype(jnp.int32) + 15, 1, 31)
    q = jnp.clip(jnp.round(x * (power(31 - k) * 0.25)), -32767.0, 32767.0)
    return q.astype(jnp.int32), 128 * (k - 1) + place + 1


def offer_kernel(volume_any, foot_any, send_ref, volume_ref, sem):
    copy = pltpu.make_async_copy(volume_any, volume_ref, sem)
    copy.start()
    copy.wait()
    send_ref[...] = jnp.broadcast_to(volume_ref[...].astype(BF16), (SHARES, 32, BLK))


def forward_kernel(slab_ref, voxel_ref, tile_ref, rows_ref, foot_ref, part_ref):
    picked = dot(slab_ref[...].reshape(1024, BLK), hot_columns(voxel_ref, 1024), SUBLANES)
    rows = rows_ref[...].reshape(1, NB)
    tile = tile_ref[...].reshape(1, NB)
    twice = lambda x: jnp.concatenate([x[:, TURNED:]] * 2, axis=1)

    lane = iota((1, BLK), 1)
    cols = jnp.concatenate([picked[:, TURNED:], jnp.ones((BLK, SET), F32)], axis=1)
    cols = jnp.concatenate([jnp.where(lane % 2 == n, cols, 0.0) for n in range(2)], axis=0).astype(BF16)
    streamed = jnp.zeros((BLK, BLK), F32)

    values = picked.T
    live = jnp.where(iota((BLK, NB), 0) < rows, 1.0, 0.0).T
    row = iota((GROUP, BLK), 0)
    one = jnp.ones((GROUP, BLK), F32)
    turned = []
    steps = TURNED // GROUP
    for g in range(steps):
        at = slice(GROUP * g, GROUP * (g + 1))
        weights = jnp.concatenate([foot_ref[k].T for k in range(at.start, at.stop)], axis=0)
        for q in range(SET // 2 * g // steps, SET // 2 * (g + 1) // steps):
            k = TURNED + 2 * q
            pair = jnp.concatenate([foot_ref[k], foot_ref[k + 1]], axis=1)
            streamed = jnp.where(lane % SET // 2 == q, dot(pair, cols), streamed)
        both = jnp.concatenate([values[at], one], axis=0)
        both_row = jnp.concatenate([row, row], axis=0)
        diag = jnp.concatenate([jnp.where(both_row == i, both, 0.0) for i in range(GROUP)], axis=1)
        out = dot(diag.astype(BF16), weights)
        turned.append(jnp.concatenate([out[:GROUP] * live[at], out[GROUP:] * live[at]], axis=1))
    tile_hot = jnp.where(iota((64, TURNED), 0) == tile[:, :TURNED], 1.0, 0.0).astype(BF16)
    first = exact_dot(tile_hot, jnp.concatenate(turned, axis=0))
    wanted = twice(tile) + jnp.where(lane < SET, 0, 64)
    tile_hot = jnp.where(iota((BLK, BLK), 0) == wanted, 1.0, 0.0).astype(BF16)
    second = exact_dot(tile_hot, jnp.where(iota((BLK, BLK), 0) < twice(rows), streamed, 0.0), LANES)
    part_ref[...] = jnp.concatenate([first[:, :BLK], first[:, BLK:]], axis=0) + second


def columns_kernel(voxel_ref, rows_ref, foot_ref, live_ref, place_ref, sums_ref, codes_ref):
    live = jnp.where(iota((BLK, NB), 0) < rows_ref[...].reshape(1, NB), 1.0, 0.0).T
    live_ref[...] = live
    place = (jnp.broadcast_to(voxel_ref[...].reshape(1, NB), (BLK, NB)) & 31).astype(F32).T.astype(jnp.int32)
    place_ref[...] = place
    sums_ref[...], codes_ref[...] = quantize(per_slot(live, foot_ref), place + 32)


def backward_kernel(voxel_any, mine_ref, left_ref, right_ref, across_ref, measured_ref, tile_ref, live_ref, place_ref, sums_ref, codes_ref, foot_ref, weighted_ref, send_ref, voxel_ref, sem):
    voxel_copy = pltpu.make_async_copy(voxel_any, voxel_ref, sem)
    voxel_copy.start()
    total = (mine_ref[...] + across_ref[...]) + (left_ref[...] + right_ref[...])
    weighted = (measured_ref[...] - total[:64]) / jnp.maximum(total[64:], 1.0)
    weighted_ref[...] = weighted
    residual = dot(hot_columns(tile_ref, 64), weighted.astype(BF16), SUBLANES) * live_ref[...]
    backs, codes = quantize(per_slot(residual, foot_ref), place_ref[...])
    send_ref[...] = jnp.zeros_like(send_ref)
    first = LINES * lax.axis_index("angle")
    line = iota((LINES, BLK), 0)
    mine = iota((LINES, BLK), 1) == (first + line) & (BLK - 1)
    spot = iota((8, BLK), 0) * BLK + iota((8, BLK), 1) - first
    spot = (spot >= 0) & (spot < LINES)
    voxel_copy.wait()
    for j in range(NB // CAP):
        at = slice(CAP * j, CAP * (j + 1))
        code = jnp.concatenate([codes[at], codes_ref[at]], axis=0)
        code = jnp.sum(jnp.where(mine, code, 0), axis=0, keepdims=True)
        code = jnp.where(spot, jnp.broadcast_to(code, (8, BLK)), 0)
        send_ref[voxel_ref[CAP * j] >> 5] = jnp.concatenate([backs[at], sums_ref[at], code], axis=0).astype(jnp.int16)


def update_kernel(recv_ref, volume_ref, weighted_ref, out_ref, weighted_out_ref):
    weighted_out_ref[...] = weighted_ref[...]
    received = recv_ref[...].astype(jnp.int32)
    codes = jnp.sum(received[:, LINES:, :], axis=0)
    scale = power(lax.shift_right_logical(codes, 7)) * 2.0**-28
    place = (codes & 127) - 1
    wanted = iota((2 * 32, BLK), 0)
    hot = jnp.concatenate(
        [
            jnp.where(place[m : m + 1, :] == wanted, jnp.broadcast_to(scale[m : m + 1, :], wanted.shape), 0.0)
            for m in range(SHARES * LINES // BLK)
        ],
        axis=1,
    ).astype(BF16)
    values = received[:, :LINES, :].astype(F32).reshape(SHARES * LINES, BLK)
    high = jnp.floor(values * (1.0 / 256.0)) * 256.0
    summed = dot(hot, high.astype(BF16)) + dot(hot, (values - high).astype(BF16))
    out_ref[...] = volume_ref[...] + summed[:32] / jnp.maximum(summed[32:], 1.0)


def call(kernel, name, out, specs, *args, scratch=()):
    out = [jax.ShapeDtypeStruct(*o) for o in out]
    return pl.pallas_call(
        kernel,
        out_shape=out,
        in_specs=specs,
        out_specs=[VMEM] * len(out),
        scratch_shapes=scratch,
        compiler_params=PARAMS,
        name=name,
    )(*args)


def on_device(volume, measured, footprint, block_voxel, block_tile, block_rows):
    (offer,) = call(
        offer_kernel,
        "offer",
        [((SHARES, 32, BLK), BF16)],
        [HBM] * 2,
        *(pltpu.with_memory_space_constraint(x, pltpu.HBM) for x in (volume, footprint)),
        scratch=[pltpu.VMEM((32, BLK), F32), pltpu.SemaphoreType.DMA],
    )
    slab_values = lax.all_to_all(offer, "angle", 0, 0)
    (part,) = call(
        forward_kernel,
        "forward",
        [((2 * 64, BLK), F32)],
        [VMEM] * 5,
        slab_values, block_voxel, block_tile, block_rows, footprint,
    )
    part = part + lax.ppermute(part, "slab", [(i, i ^ 1) for i in range(8)])
    left = lax.ppermute(part, "slab", [(i, i ^ 2) for i in range(8)])
    right = lax.ppermute(part, "slab", [(i, 6 - i + 2 * (i % 2)) for i in range(8)])
    across = lax.ppermute(part, "slab", [(i, i ^ 4) for i in range(8)])
    live, place, column_sums, column_codes = call(
        columns_kernel,
        "columns",
        [((NB, BLK), F32)] + [((NB, BLK), jnp.int32)] * 3,
        [VMEM] * 3,
        block_voxel, block_rows, footprint,
    )
    weighted, send_back = call(
        backward_kernel,
        "backward",
        [((64, BLK), F32), ((SHARES, 32, BLK), jnp.int16)],
        [VMEM] * 12,
        block_voxel, part, left, right, across, measured, block_tile, live, place, column_sums, column_codes, footprint,
        scratch=[pltpu.SMEM((NB,), jnp.int32), pltpu.SemaphoreType.DMA],
    )
    received = lax.all_to_all(send_back, "angle", 0, 0)
    return call(
        update_kernel,
        "update",
        [((32, BLK), F32), ((64, BLK), F32)],
        [VMEM] * 3,
        received, volume, weighted,
    )


def solution(mesh):
    in_specs = (
        P(("slab", "angle"), None),
        P("angle", None),
        P(("slab", "angle"), None, None),
        P(("slab", "angle")),
        P(("slab", "angle")),
        P(("slab", "angle")),
    )
    out_specs = (P(("slab", "angle"), None), P("angle", None))
    return jax.shard_map(
        on_device, mesh=mesh, in_specs=in_specs, out_specs=out_specs, check_vma=False
    )
```

```python
import jax
import jax.numpy as jnp
from jax import lax
from jax.experimental import pallas as pl
from jax.experimental.pallas import tpu as pltpu
from jax.sharding import PartitionSpec as P

BLK = 128
NB = 192
CAP = 12
SHARES = 32
GROUP = 16
TURNED = 128
SET = NB - TURNED
LINES = 2 * CAP
PAD = 16
F32 = jnp.float32
BF16 = jnp.bfloat16
VMEM = pl.BlockSpec(memory_space=pltpu.VMEM)
HBM = pl.BlockSpec(memory_space=pltpu.HBM)
PARAMS = pltpu.CompilerParams(vmem_limit_bytes=40 * 1024 * 1024)
ROWS = ((1,), (0,))
LANES = ((1,), (1,))
SUBLANES = ((0,), (0,))


def dot(a, b, contract=ROWS):
    return lax.dot_general(a, b, (contract, ((), ())), preferred_element_type=F32)


def iota(shape, dim):
    return lax.broadcasted_iota(jnp.int32, shape, dim)


def exact_dot(onehot, x, contract=ROWS):
    hi = x.astype(BF16)
    rest = x - hi.astype(F32)
    mid = rest.astype(BF16)
    lo = (rest - mid.astype(F32)).astype(BF16)
    return dot(onehot, hi, contract) + (dot(onehot, mid, contract) + dot(onehot, lo, contract))


def per_slot(vectors, matrices, group=GROUP):
    row = iota((group, BLK), 0)
    out = []
    for g in range(0, NB, group):
        mine = vectors[g : g + group]
        diag = jnp.concatenate([jnp.where(row == i, mine, 0.0) for i in range(group)], axis=1).astype(BF16)
        out.append(dot(diag, matrices[g : g + group].reshape(group * BLK, BLK)))
    return jnp.concatenate(out, axis=0)


def hot_columns(ref, n):
    return jnp.where(iota((n, NB), 0) == ref[...].reshape(1, NB), 1.0, 0.0).astype(BF16)


def power(k):
    return lax.shift_left(jnp.ones_like(k), k).astype(F32)


def quantize(x, place):
    largest = jnp.max(jnp.abs(x), axis=1, keepdims=True)
    k = jnp.clip(jnp.floor(jnp.log2(jnp.maximum(largest, 2.0**-20))).astype(jnp.int32) + 15, 1, 31)
    q = jnp.clip(jnp.round(x * (power(31 - k) * 0.25)), -32767.0, 32767.0)
    return q.astype(jnp.int32), 128 * (k - 1) + place + 1


def offer_kernel(volume_any, foot_any, send_ref, volume_ref, sem):
    copy = pltpu.make_async_copy(volume_any, volume_ref, sem)
    copy.start()
    copy.wait()
    send_ref[...] = jnp.broadcast_to(volume_ref[...].astype(BF16), (SHARES, 32, BLK))


def forward_kernel(slab_ref, voxel_ref, tile_ref, rows_ref, foot_ref, part_ref):
    picked = dot(slab_ref[...].reshape(1024, BLK), hot_columns(voxel_ref, 1024), SUBLANES)
    rows = rows_ref[...].reshape(1, NB)
    tile = tile_ref[...].reshape(1, NB)
    twice = lambda x: jnp.concatenate([x[:, TURNED:]] * 2, axis=1)

    lane = iota((1, BLK), 1)
    cols = jnp.concatenate([picked[:, TURNED:], jnp.ones((BLK, SET), F32)], axis=1)
    cols = jnp.concatenate([jnp.where(lane % 2 == n, cols, 0.0) for n in range(2)], axis=0).astype(BF16)
    streamed = jnp.zeros((BLK, BLK), F32)

    values = picked.T
    live = jnp.where(iota((BLK, NB), 0) < rows, 1.0, 0.0).T
    row = iota((GROUP, BLK), 0)
    one = jnp.ones((GROUP, BLK), F32)
    turned = []
    steps = TURNED // GROUP
    for g in range(steps):
        at = slice(GROUP * g, GROUP * (g + 1))
        weights = jnp.concatenate([foot_ref[k].T for k in range(at.start, at.stop)], axis=0)
        for q in range(SET // 2 * g // steps, SET // 2 * (g + 1) // steps):
            k = TURNED + 2 * q
            pair = jnp.concatenate([foot_ref[k], foot_ref[k + 1]], axis=1)
            streamed = jnp.where(lane % SET // 2 == q, dot(pair, cols), streamed)
        both = jnp.concatenate([values[at], one], axis=0)
        both_row = jnp.concatenate([row, row], axis=0)
        diag = jnp.concatenate([jnp.where(both_row == i, both, 0.0) for i in range(GROUP)], axis=1)
        out = dot(diag.astype(BF16), weights)
        turned.append(jnp.concatenate([out[:GROUP] * live[at], out[GROUP:] * live[at]], axis=1))
    tile_hot = jnp.where(iota((64, TURNED), 0) == tile[:, :TURNED], 1.0, 0.0).astype(BF16)
    first = exact_dot(tile_hot, jnp.concatenate(turned, axis=0))
    wanted = twice(tile) + jnp.where(lane < SET, 0, 64)
    tile_hot = jnp.where(iota((BLK, BLK), 0) == wanted, 1.0, 0.0).astype(BF16)
    second = exact_dot(tile_hot, jnp.where(iota((BLK, BLK), 0) < twice(rows), streamed, 0.0), LANES)
    part_ref[...] = jnp.concatenate([first[:, :BLK], first[:, BLK:]], axis=0) + second


def padded(x):
    gap = jnp.zeros((PAD - CAP, x.shape[1]), x.dtype)
    return jnp.concatenate([y for j in range(NB // CAP) for y in (x[CAP * j : CAP * (j + 1)], gap)], axis=0)


def own_lanes(count, start):
    first = LINES * lax.axis_index("angle") + start
    line = iota((PAD, BLK), 0)
    mine = (iota((PAD, BLK), 1) == (first + line) & (BLK - 1)) & (line < count)
    spot = iota((8, BLK), 0) * BLK + iota((8, BLK), 1) - first
    return mine, (spot >= 0) & (spot < count)


def code_rows(code, mine, spot):
    code = jnp.sum(jnp.where(mine, code, 0), axis=0, keepdims=True)
    return jnp.where(spot, jnp.broadcast_to(code, spot.shape), 0)


def columns_kernel(voxel_ref, tile_ref, rows_ref, foot_ref, live_ref, place_ref, hot_ref, block_ref):
    live = jnp.where(iota((BLK, NB), 0) < rows_ref[...].reshape(1, NB), 1.0, 0.0).T
    live_ref[...] = padded(live)
    turned = lambda ref: jnp.broadcast_to(ref[...].reshape(1, NB), (BLK, NB)).astype(F32).T.astype(jnp.int32)
    place = padded(turned(voxel_ref) & 31)
    place_ref[...] = place
    tile = padded(turned(tile_ref) + 1) - 1
    hot_ref[...] = jnp.where(tile[:, :64] == iota((PAD * NB // CAP, 64), 1), 1.0, 0.0).astype(BF16)
    sums, codes = quantize(padded(per_slot(live, foot_ref)), place + 32)
    mine, spot = own_lanes(CAP, CAP)
    none = jnp.zeros((CAP, BLK), jnp.int32)
    for j in range(NB // CAP):
        at = slice(PAD * j, PAD * (j + 1))
        code = code_rows(codes[at], mine, spot)
        block_ref[j] = jnp.concatenate([none, sums[at][:CAP], code], axis=0)


def backward_kernel(voxel_any, mine_ref, left_ref, right_ref, across_ref, measured_ref, live_ref, place_ref, hot_ref, block_ref, foot_ref, weighted_ref, send_ref, voxel_ref, sem):
    voxel_copy = pltpu.make_async_copy(voxel_any, voxel_ref, sem)
    voxel_copy.start()
    total = (mine_ref[...] + across_ref[...]) + (left_ref[...] + right_ref[...])
    weighted = (measured_ref[...] - total[:64]) / jnp.maximum(total[64:], 1.0)
    weighted_ref[...] = weighted
    residual = dot(hot_ref[...], weighted.astype(BF16)) * live_ref[...]
    send_ref[...] = jnp.zeros_like(send_ref)
    mine, spot = own_lanes(CAP, 0)
    row = iota((PAD, BLK), 0)
    none = jnp.zeros((8, BLK), jnp.int32)

    def product(j):
        vectors = residual[PAD * j : PAD * (j + 1)]
        diag = jnp.concatenate([jnp.where(row == i, vectors, 0.0) for i in range(CAP)], axis=1).astype(BF16)
        return dot(diag, foot_ref[CAP * j : CAP * (j + 1)].reshape(CAP * BLK, BLK))

    products = [product(j) for j in range(NB // CAP)]
    blocks = []
    for j in range(NB // CAP):
        back, code = quantize(products[j], place_ref[PAD * j : PAD * (j + 1)])
        block = jnp.concatenate([back, none, code_rows(code, mine, spot)], axis=0) + block_ref[j]
        blocks.append(block.astype(jnp.int16))
    voxel_copy.wait()
    for j in range(NB // CAP):
        send_ref[voxel_ref[CAP * j] >> 5] = blocks[j]


def update_kernel(recv_ref, volume_ref, weighted_ref, out_ref, weighted_out_ref):
    weighted_out_ref[...] = weighted_ref[...]
    received = recv_ref[...].astype(jnp.int32)
    codes = jnp.sum(received[:, LINES:, :], axis=0)
    scale = power(lax.shift_right_logical(codes, 7)) * 2.0**-28
    place = (codes & 127) - 1
    wanted = iota((2 * 32, BLK), 0)
    hot = jnp.concatenate(
        [
            jnp.where(place[m : m + 1, :] == wanted, jnp.broadcast_to(scale[m : m + 1, :], wanted.shape), 0.0)
            for m in range(SHARES * LINES // BLK)
        ],
        axis=1,
    ).astype(BF16)
    values = received[:, :LINES, :].astype(F32).reshape(SHARES * LINES, BLK)
    high = jnp.floor(values * (1.0 / 256.0)) * 256.0
    summed = dot(hot, high.astype(BF16)) + dot(hot, (values - high).astype(BF16))
    out_ref[...] = volume_ref[...] + summed[:32] / jnp.maximum(summed[32:], 1.0)


def call(kernel, name, out, specs, *args, scratch=()):
    out = [jax.ShapeDtypeStruct(*o) for o in out]
    return pl.pallas_call(
        kernel,
        out_shape=out,
        in_specs=specs,
        out_specs=[VMEM] * len(out),
        scratch_shapes=scratch,
        compiler_params=PARAMS,
        name=name,
    )(*args)


def on_device(volume, measured, footprint, block_voxel, block_tile, block_rows):
    (offer,) = call(
        offer_kernel,
        "offer",
        [((SHARES, 32, BLK), BF16)],
        [HBM] * 2,
        *(pltpu.with_memory_space_constraint(x, pltpu.HBM) for x in (volume, footprint)),
        scratch=[pltpu.VMEM((32, BLK), F32), pltpu.SemaphoreType.DMA],
    )
    slab_values = lax.all_to_all(offer, "angle", 0, 0)
    (part,) = call(
        forward_kernel,
        "forward",
        [((2 * 64, BLK), F32)],
        [VMEM] * 5,
        slab_values, block_voxel, block_tile, block_rows, footprint,
    )
    part = part + lax.ppermute(part, "slab", [(i, i ^ 1) for i in range(8)])
    left = lax.ppermute(part, "slab", [(i, i ^ 2) for i in range(8)])
    right = lax.ppermute(part, "slab", [(i, 6 - i + 2 * (i % 2)) for i in range(8)])
    across = lax.ppermute(part, "slab", [(i, i ^ 4) for i in range(8)])
    live, place, tile_hot, blocks = call(
        columns_kernel,
        "columns",
        [((256, BLK), F32), ((256, BLK), jnp.int32), ((256, 64), BF16), ((NB // CAP, 32, BLK), jnp.int32)],
        [VMEM] * 4,
        block_voxel, block_tile, block_rows, footprint,
    )
    weighted, send_back = call(
        backward_kernel,
        "backward",
        [((64, BLK), F32), ((SHARES, 32, BLK), jnp.int16)],
        [VMEM] * 11,
        block_voxel, part, left, right, across, measured, live, place, tile_hot, blocks, footprint,
        scratch=[pltpu.SMEM((NB,), jnp.int32), pltpu.SemaphoreType.DMA],
    )
    received = lax.all_to_all(send_back, "angle", 0, 0)
    return call(
        update_kernel,
        "update",
        [((32, BLK), F32), ((64, BLK), F32)],
        [VMEM] * 3,
        received, volume, weighted,
    )


def solution(mesh):
    in_specs = (
        P(("slab", "angle"), None),
        P("angle", None),
        P(("slab", "angle"), None, None),
        P(("slab", "angle")),
        P(("slab", "angle")),
        P(("slab", "angle")),
    )
    out_specs = (P(("slab", "angle"), None), P("angle", None))
    return jax.shard_map(
        on_device, mesh=mesh, in_specs=in_specs, out_specs=out_specs, check_vma=False
    )
```

```python
import jax
import jax.numpy as jnp
from jax import lax
from jax.experimental import pallas as pl
from jax.experimental.pallas import tpu as pltpu
from jax.sharding import PartitionSpec as P

BLK = 128
NB = 192
CAP = 12
SHARES = 32
GROUP = 16
TURNED = 128
SET = NB - TURNED
LINES = 2 * CAP
PAD = 16
F32 = jnp.float32
BF16 = jnp.bfloat16
VMEM = pl.BlockSpec(memory_space=pltpu.VMEM)
HBM = pl.BlockSpec(memory_space=pltpu.HBM)
PARAMS = pltpu.CompilerParams(vmem_limit_bytes=40 * 1024 * 1024)
ROWS = ((1,), (0,))
LANES = ((1,), (1,))
SUBLANES = ((0,), (0,))


def dot(a, b, contract=ROWS):
    return lax.dot_general(a, b, (contract, ((), ())), preferred_element_type=F32)


def iota(shape, dim):
    return lax.broadcasted_iota(jnp.int32, shape, dim)


def exact_dot(onehot, x, contract=ROWS):
    hi = x.astype(BF16)
    rest = x - hi.astype(F32)
    mid = rest.astype(BF16)
    lo = (rest - mid.astype(F32)).astype(BF16)
    return dot(onehot, hi, contract) + (dot(onehot, mid, contract) + dot(onehot, lo, contract))


def per_slot(vectors, matrices, group=GROUP):
    row = iota((group, BLK), 0)
    out = []
    for g in range(0, NB, group):
        mine = vectors[g : g + group]
        diag = jnp.concatenate([jnp.where(row == i, mine, 0.0) for i in range(group)], axis=1).astype(BF16)
        out.append(dot(diag, matrices[g : g + group].reshape(group * BLK, BLK)))
    return jnp.concatenate(out, axis=0)


def hot_columns(ref, n):
    return jnp.where(iota((n, NB), 0) == ref[...].reshape(1, NB), 1.0, 0.0).astype(BF16)


def power(k):
    return lax.shift_left(jnp.ones_like(k), k).astype(F32)


def quantize(x, place):
    largest = jnp.max(jnp.abs(x), axis=1, keepdims=True)
    k = jnp.clip(jnp.floor(jnp.log2(jnp.maximum(largest, 2.0**-20))).astype(jnp.int32) + 15, 1, 31)
    q = jnp.clip(jnp.round(x * (power(31 - k) * 0.25)), -32767.0, 32767.0)
    return q.astype(jnp.int32), 128 * (k - 1) + place + 1


def offer_kernel(volume_any, foot_any, send_ref, volume_ref, sem):
    copy = pltpu.make_async_copy(volume_any, volume_ref, sem)
    copy.start()
    copy.wait()
    send_ref[...] = jnp.broadcast_to(volume_ref[...].astype(BF16), (SHARES, 32, BLK))


def forward_kernel(slab_ref, voxel_ref, tile_ref, rows_ref, foot_ref, part_ref):
    picked = dot(slab_ref[...].reshape(1024, BLK), hot_columns(voxel_ref, 1024), SUBLANES)
    rows = rows_ref[...].reshape(1, NB)
    tile = tile_ref[...].reshape(1, NB)
    twice = lambda x: jnp.concatenate([x[:, TURNED:]] * 2, axis=1)

    lane = iota((1, BLK), 1)
    cols = jnp.concatenate([picked[:, TURNED:], jnp.ones((BLK, SET), F32)], axis=1)
    cols = jnp.concatenate([jnp.where(lane % 2 == n, cols, 0.0) for n in range(2)], axis=0).astype(BF16)
    streamed = jnp.zeros((BLK, BLK), F32)

    values = picked.T
    live = jnp.where(iota((BLK, NB), 0) < rows, 1.0, 0.0).T
    row = iota((GROUP, BLK), 0)
    one = jnp.ones((GROUP, BLK), F32)
    turned = []
    steps = TURNED // GROUP
    for g in range(steps):
        at = slice(GROUP * g, GROUP * (g + 1))
        weights = jnp.concatenate([foot_ref[k].T for k in range(at.start, at.stop)], axis=0)
        for q in range(SET // 2 * g // steps, SET // 2 * (g + 1) // steps):
            k = TURNED + 2 * q
            pair = jnp.concatenate([foot_ref[k], foot_ref[k + 1]], axis=1)
            streamed = jnp.where(lane % SET // 2 == q, dot(pair, cols), streamed)
        both = jnp.concatenate([values[at], one], axis=0)
        both_row = jnp.concatenate([row, row], axis=0)
        diag = jnp.concatenate([jnp.where(both_row == i, both, 0.0) for i in range(GROUP)], axis=1)
        out = dot(diag.astype(BF16), weights)
        turned.append(jnp.concatenate([out[:GROUP] * live[at], out[GROUP:] * live[at]], axis=1))
    tile_hot = jnp.where(iota((64, TURNED), 0) == tile[:, :TURNED], 1.0, 0.0).astype(BF16)
    first = exact_dot(tile_hot, jnp.concatenate(turned, axis=0))
    wanted = twice(tile) + jnp.where(lane < SET, 0, 64)
    tile_hot = jnp.where(iota((BLK, BLK), 0) == wanted, 1.0, 0.0).astype(BF16)
    second = exact_dot(tile_hot, jnp.where(iota((BLK, BLK), 0) < twice(rows), streamed, 0.0), LANES)
    part_ref[...] = jnp.concatenate([first[:, :BLK], first[:, BLK:]], axis=0) + second


def padded(x):
    gap = jnp.zeros((PAD - CAP, x.shape[1]), x.dtype)
    return jnp.concatenate([y for j in range(NB // CAP) for y in (x[CAP * j : CAP * (j + 1)], gap)], axis=0)


def own_lanes(count, start):
    first = LINES * lax.axis_index("angle") + start
    line = iota((PAD, BLK), 0)
    mine = (iota((PAD, BLK), 1) == (first + line) & (BLK - 1)) & (line < count)
    spot = iota((8, BLK), 0) * BLK + iota((8, BLK), 1) - first
    return mine, (spot >= 0) & (spot < count)


def code_rows(code, mine, spot):
    code = jnp.sum(jnp.where(mine, code, 0), axis=0, keepdims=True)
    return jnp.where(spot, jnp.broadcast_to(code, spot.shape), 0)


def columns_kernel(voxel_ref, tile_ref, rows_ref, foot_ref, live_ref, place_ref, hot_ref, block_ref):
    live = jnp.where(iota((BLK, NB), 0) < rows_ref[...].reshape(1, NB), 1.0, 0.0).T
    live_ref[...] = padded(live)
    turned = lambda ref: jnp.broadcast_to(ref[...].reshape(1, NB), (BLK, NB)).astype(F32).T.astype(jnp.int32)
    place = padded(turned(voxel_ref) & 31)
    place_ref[...] = place
    tile = padded(turned(tile_ref) + 1) - 1
    hot_ref[...] = jnp.where(tile[:, :64] == iota((PAD * NB // CAP, 64), 1), 1.0, 0.0).astype(BF16)
    sums, codes = quantize(padded(per_slot(live, foot_ref)), place + 32)
    mine, spot = own_lanes(CAP, CAP)
    none = jnp.zeros((CAP, BLK), jnp.int32)
    for j in range(NB // CAP):
        at = slice(PAD * j, PAD * (j + 1))
        code = code_rows(codes[at], mine, spot)
        block_ref[j] = jnp.concatenate([none, sums[at][:CAP], code], axis=0)


def backward_kernel(voxel_any, mine_ref, left_ref, across_ref, right_ref, measured_ref, live_ref, place_ref, hot_ref, block_ref, foot_ref, weighted_ref, send_ref, voxel_ref, sem):
    voxel_copy = pltpu.make_async_copy(voxel_any, voxel_ref, sem)
    voxel_copy.start()
    total = (mine_ref[...] + across_ref[...]) + (left_ref[...] + right_ref[...])
    weighted = (measured_ref[...] - total[:64]) / jnp.maximum(total[64:], 1.0)
    weighted_ref[...] = weighted
    residual = dot(hot_ref[...], weighted.astype(BF16)) * live_ref[...]
    send_ref[...] = jnp.zeros_like(send_ref)
    mine, spot = own_lanes(CAP, 0)
    row = iota((PAD, BLK), 0)
    none = jnp.zeros((8, BLK), jnp.int32)

    def product(j):
        vectors = residual[PAD * j : PAD * (j + 1)]
        diag = jnp.concatenate([jnp.where(row == i, vectors, 0.0) for i in range(CAP)], axis=1).astype(BF16)
        return dot(diag, foot_ref[CAP * j : CAP * (j + 1)].reshape(CAP * BLK, BLK))

    products = [product(j) for j in range(NB // CAP)]
    blocks = []
    for j in range(NB // CAP):
        back, code = quantize(products[j], place_ref[PAD * j : PAD * (j + 1)])
        block = jnp.concatenate([back, none, code_rows(code, mine, spot)], axis=0) + block_ref[j]
        blocks.append(block.astype(jnp.int16))
    voxel_copy.wait()
    for j in range(NB // CAP):
        send_ref[voxel_ref[CAP * j] >> 5] = blocks[j]


def update_kernel(recv_ref, volume_ref, weighted_ref, out_ref, weighted_out_ref):
    weighted_out_ref[...] = weighted_ref[...]
    received = recv_ref[...].astype(jnp.int32)
    codes = jnp.sum(received[:, LINES:, :], axis=0)
    scale = power(lax.shift_right_logical(codes, 7)) * 2.0**-28
    place = (codes & 127) - 1
    wanted = iota((2 * 32, BLK), 0)
    hot = jnp.concatenate(
        [
            jnp.where(place[m : m + 1, :] == wanted, jnp.broadcast_to(scale[m : m + 1, :], wanted.shape), 0.0)
            for m in range(SHARES * LINES // BLK)
        ],
        axis=1,
    ).astype(BF16)
    values = received[:, :LINES, :].astype(F32).reshape(SHARES * LINES, BLK)
    high = jnp.floor(values * (1.0 / 256.0)) * 256.0
    summed = dot(hot, high.astype(BF16)) + dot(hot, (values - high).astype(BF16))
    out_ref[...] = volume_ref[...] + summed[:32] / jnp.maximum(summed[32:], 1.0)


def call(kernel, name, out, specs, *args, scratch=()):
    out = [jax.ShapeDtypeStruct(*o) for o in out]
    return pl.pallas_call(
        kernel,
        out_shape=out,
        in_specs=specs,
        out_specs=[VMEM] * len(out),
        scratch_shapes=scratch,
        compiler_params=PARAMS,
        name=name,
    )(*args)


def on_device(volume, measured, footprint, block_voxel, block_tile, block_rows):
    (offer,) = call(
        offer_kernel,
        "offer",
        [((SHARES, 32, BLK), BF16)],
        [HBM] * 2,
        *(pltpu.with_memory_space_constraint(x, pltpu.HBM) for x in (volume, footprint)),
        scratch=[pltpu.VMEM((32, BLK), F32), pltpu.SemaphoreType.DMA],
    )
    slab_values = lax.all_to_all(offer, "angle", 0, 0)
    (part,) = call(
        forward_kernel,
        "forward",
        [((2 * 64, BLK), F32)],
        [VMEM] * 5,
        slab_values, block_voxel, block_tile, block_rows, footprint,
    )
    part = part + lax.ppermute(part, "slab", [(i, i ^ 1) for i in range(8)])
    left = lax.ppermute(part, "slab", [(i, i ^ 2) for i in range(8)])
    right = lax.ppermute(part, "slab", [(i, 6 - i + 2 * (i % 2)) for i in range(8)])
    across = lax.ppermute(part, "slab", [(i, i ^ 4) for i in range(8)])
    live, place, tile_hot, blocks = call(
        columns_kernel,
        "columns",
        [((256, BLK), F32), ((256, BLK), jnp.int32), ((256, 64), BF16), ((NB // CAP, 32, BLK), jnp.int32)],
        [VMEM] * 4,
        block_voxel, block_tile, block_rows, footprint,
    )
    weighted, send_back = call(
        backward_kernel,
        "backward",
        [((64, BLK), F32), ((SHARES, 32, BLK), jnp.int16)],
        [VMEM] * 11,
        block_voxel, part, left, across, right, measured, live, place, tile_hot, blocks, footprint,
        scratch=[pltpu.SMEM((NB,), jnp.int32), pltpu.SemaphoreType.DMA],
    )
    received = lax.all_to_all(send_back, "angle", 0, 0)
    return call(
        update_kernel,
        "update",
        [((32, BLK), F32), ((64, BLK), F32)],
        [VMEM] * 3,
        received, volume, weighted,
    )


def solution(mesh):
    in_specs = (
        P(("slab", "angle"), None),
        P("angle", None),
        P(("slab", "angle"), None, None),
        P(("slab", "angle")),
        P(("slab", "angle")),
        P(("slab", "angle")),
    )
    out_specs = (P(("slab", "angle"), None), P("angle", None))
    return jax.shard_map(
        on_device, mesh=mesh, in_specs=in_specs, out_specs=out_specs, check_vma=False
    )
```
